256 devices in a mesh: section: 32 (over x, z_hi, y), dp: 8 (over z_lo, core).
Axes of the slice: x: 4, y: 4, z: 8 (z_hi: 2, z_lo: 4; z = z_hi * 4 + z_lo), core: 2. Of those that a mesh axis runs over, the one named last changes fastest.
Arguments:
- saved_entering_lanes: bfloat16 [32, 2, 1024, 4, 1024], P('section', None, 'dp'), may hold values from -6 to 6
- opening_adjoint: bfloat16 [32, 1024, 4, 1024], P('section', 'dp'), may hold values from -6 to 6
- final_later_adjoint: bfloat16 [1, 1024, 4, 1024], P(None, 'dp'), may hold values from -6 to 6
- document_labels: int32 [32, 2, 1024], P('section', None, 'dp'), may hold values from 0 to 63, never falling along the last dimension, each value on 1 to 48 neighbouring positions
- blend_linear_map: float32 [32, 4096, 24], P('section'), may hold values from -0.1875 to 0.1875
- rescale_amplitude: float32 [32, 1024], P('section'), may hold values from 0.5 to 1.5
- attend_entry_maps: bfloat16 [32, 1024, 1536], P('section'), may hold values from -0.1875 to 0.1875
- attend_exit_map: bfloat16 [32, 512, 1024], P('section'), may hold values from -0.25 to 0.25
Outputs:
- sent: bfloat16 [32, 2, 1024, 4, 1024], P('section', None, 'dp')
- grad_qkv: float32 [32, 1024, 1536], P('section', 'dp')
- grad_out: float32 [32, 512, 1024], P('section', 'dp')
- grad_proj: float32 [32, 4096, 24], P('section', 'dp')
- grad_gain: float32 [32, 1024], P('section', 'dp')
The draws below stay inside these ranges and needn't reach their ends.
Inputs may be any that keep to these rules, and one draw needn't show every extreme that they name: `document_labels`: along a microbatch's row of 1024 tokens the segment ids never fall.
All inputs are finite; a program needn't handle non-finite values.
Results may differ from the reference program's by a relative error of at most 0.03.
Values may be sent and summed in bfloat16 or wider, within the bound.
No kernel may reach another device: no remote copies, remote signals or barrier semaphores. Data moves between devices by JAX's collectives and lax.ppermute only.
A program may use at most 128 MiB of HBM per device.

```python
import math
import jax
import jax.numpy as jnp
import numpy as np
from jax import lax

HIDDEN_WIDTH = 1024
SKIP_LANES = 4
HEADS = 8
HEAD_DIM = 64
TOK = 128
TICKS = 2
SINK = 20
COEFS = 24
DEPTH_PARTS = 32
WORDS_PER_STEP = 1024
N_DP = 8


def levels(key, dims, cuts, low, largest):
    factor_of = 1.0
    for axis_at, parts in cuts:
        heights = jax.random.uniform(jax.random.fold_in(jax.random.fold_in(key, 6), axis_at), (parts,), jnp.float32, low / len(cuts), largest / len(cuts))
        factor_of = factor_of * jnp.repeat(jnp.exp(heights), dims[axis_at] // parts).reshape((-1,) + (1,) * (len(dims) - 1 - axis_at))
    return factor_of


def length_profile(amount, total, most, slope):
    weights = [(1 << 20) // math.isqrt(standing ** slope) + 1 for standing in range(2, amount + 1)]
    spare, holding = total - most - (amount - 1), [1] * (amount - 1)
    while spare > 0:
        movable = [i for i in range(amount - 1) if holding[i] < most]
        mass, budget = sum([weights[i] for i in movable]), spare
        for i in movable:
            extra = min(most - holding[i], max(1, budget * weights[i] // mass), spare)
            holding[i] = holding[i] + extra
            spare = spare - extra
    return np.array([most] + holding)


def uneven_parts(own_key, amount, total, reach, lean):
    if amount == 2:
        one = jax.random.randint(own_key, (), max(1, total - reach), min(reach, total - 1) + 1)
        return jnp.stack([one, total - one])
    sizes = jnp.asarray(length_profile(amount, total, reach, lean), jnp.int32)
    twos = (amount - 1) // 2
    donor, receiver = sizes[1:1 + 2 * twos:2], sizes[2:2 + 2 * twos:2]
    slack = jnp.minimum(donor - 1, reach - receiver)
    moved = jax.random.randint(jax.random.fold_in(own_key, 1), (twos,), 0, 1 << 20) % (slack + 1)
    sizes = sizes.at[1:1 + 2 * twos:2].set(donor - moved).at[2:2 + 2 * twos:2].set(receiver + moved)
    return sizes[jax.random.permutation(jax.random.fold_in(own_key, 2), amount)]


def bell_draw(rng, extent, spread, limit, cuts=(), held_as=jnp.bfloat16):
    values = spread * jax.random.normal(rng, extent, jnp.float32)
    if cuts:
        values = values * levels(rng, extent, cuts, -0.22, 0.18)
    return jnp.clip(values, -limit, limit).astype(held_as)


def setup_inputs(seed: int = 0) -> dict:
    streams_of = jax.random.split(jax.random.key(seed), 9)
    return {
        "saved_entering_lanes": bell_draw(streams_of[0], (DEPTH_PARTS, TICKS, WORDS_PER_STEP, SKIP_LANES, HIDDEN_WIDTH), 1.0, 6.0, ((0, 32), (2, 8))),
        "opening_adjoint": bell_draw(streams_of[1], (DEPTH_PARTS, WORDS_PER_STEP, SKIP_LANES, HIDDEN_WIDTH), 1.0, 6.0, ((0, 32), (1, 8))),
        "final_later_adjoint": bell_draw(streams_of[2], (TICKS - 1, WORDS_PER_STEP, SKIP_LANES, HIDDEN_WIDTH), 1.0, 6.0, ((1, 8),)),
        "document_labels": jax.vmap(lambda own: jnp.searchsorted(jnp.cumsum(uneven_parts(own, WORDS_PER_STEP // 16, WORDS_PER_STEP, 48, 1)), jnp.arange(WORDS_PER_STEP), side="right"))(jax.random.split(streams_of[3], DEPTH_PARTS * TICKS)).reshape((DEPTH_PARTS, TICKS, WORDS_PER_STEP)).astype(jnp.int32),
        "blend_linear_map": bell_draw(streams_of[4], (DEPTH_PARTS, SKIP_LANES * HIDDEN_WIDTH, COEFS), HIDDEN_WIDTH ** -0.5, 0.1875, ((0, 32),), jnp.float32),
        "rescale_amplitude": jnp.clip(1.0 + 0.1 * jax.random.normal(streams_of[5], (DEPTH_PARTS, HIDDEN_WIDTH), jnp.float32), 0.5, 1.5),
        "attend_entry_maps": bell_draw(streams_of[6], (DEPTH_PARTS, HIDDEN_WIDTH, 3 * HEADS * HEAD_DIM), HIDDEN_WIDTH ** -0.5, 0.1875, ((0, 32),)),
        "attend_exit_map": bell_draw(streams_of[7], (DEPTH_PARTS, HEADS * HEAD_DIM, HIDDEN_WIDTH), (HEADS * HEAD_DIM) ** -0.5, 0.25, ((0, 32),)),
    }


def doubly_stochastic_normalize(mixing_matrix):

    def one_round(index_val, current):
        current = current / lax.optimization_barrier(jnp.sum(current, axis=1, keepdims=True))
        return current / lax.optimization_barrier(jnp.sum(current, axis=0, keepdims=True))
    return lax.fori_loop(0, SINK, one_round, mixing_matrix)

def head_norm(block):
    widened = block.astype(jnp.float32)
    return (widened * lax.rsqrt(lax.optimization_barrier(jnp.mean(widened * widened, axis=-1, keepdims=True)) + 1e-06)).astype(jnp.bfloat16)

def stream_layer(streams, segment_ids, blend_linear_map, rescale_amplitude, attend_entry_maps, attend_exit_map, qkv_hole, att_hole):
    batch_groups, sequence_length, residual_stream_count, model_width = streams.shape
    widened = streams.astype(jnp.float32)
    flattened = widened.reshape(batch_groups * sequence_length, residual_stream_count * model_width)
    inv_scale = lax.rsqrt(lax.optimization_barrier(jnp.mean(flattened * flattened, axis=-1, keepdims=True)) + 1e-06)
    mixing_coefficient = jnp.dot(flattened * inv_scale, blend_linear_map, precision=lax.Precision.HIGHEST).reshape(batch_groups, sequence_length, -1)
    pre_gate = jax.nn.sigmoid(mixing_coefficient[..., :residual_stream_count])
    post_gate = 2.0 * jax.nn.sigmoid(mixing_coefficient[..., residual_stream_count:2 * residual_stream_count])
    raw_mix = jnp.exp(mixing_coefficient[..., 2 * residual_stream_count:]).reshape(batch_groups * sequence_length, residual_stream_count, residual_stream_count)
    settled = doubly_stochastic_normalize(jnp.transpose(raw_mix, (1, 2, 0)))
    stream_mixing = jnp.transpose(settled, (2, 0, 1)).reshape(batch_groups, sequence_length, residual_stream_count, residual_stream_count)
    joined = lax.optimization_barrier(jnp.sum(pre_gate[..., None] * widened, axis=2))
    normed = (joined * lax.rsqrt(lax.optimization_barrier(jnp.mean(joined * joined, axis=-1, keepdims=True)) + 1e-06) * rescale_amplitude).astype(jnp.bfloat16)
    projected = jnp.dot(normed.reshape(-1, model_width), attend_entry_maps, preferred_element_type=jnp.float32)
    projected = projected.astype(jnp.bfloat16).reshape(batch_groups, sequence_length, -1) + qkv_hole
    inner = attend_entry_maps.shape[1] // 3
    queries = head_norm(projected[..., :inner].reshape(batch_groups, sequence_length, -1, HEAD_DIM))
    key_vecs = head_norm(projected[..., inner:2 * inner].reshape(batch_groups, sequence_length, -1, HEAD_DIM))
    val_vecs = projected[..., 2 * inner:].reshape(batch_groups, sequence_length, -1, HEAD_DIM)
    scores = jnp.einsum('bqhe,bkhe->bhqk', queries.astype(jnp.float32), key_vecs.astype(jnp.float32)) * (1.0 / math.sqrt(HEAD_DIM))
    positions = jnp.arange(sequence_length)
    allowed = (segment_ids[:, :, None] == segment_ids[:, None, :]) & (positions[None, None, :] <= positions[None, :, None])
    unnormed = jnp.where(allowed[:, None], jnp.exp(scores), 0.0)
    weights = (unnormed / lax.optimization_barrier(jnp.sum(unnormed, axis=-1, keepdims=True))).astype(jnp.bfloat16)
    context = jnp.einsum('bhqk,bkhe->bqhe', weights.astype(jnp.float32), val_vecs.astype(jnp.float32))
    context = context.astype(jnp.bfloat16).reshape(batch_groups, sequence_length, inner)
    attended = jnp.dot(context.reshape(-1, inner), attend_exit_map, preferred_element_type=jnp.float32).reshape(batch_groups, sequence_length, model_width) + att_hole
    carried = post_gate[..., None] * attended[:, :, None, :]
    for source in range(residual_stream_count):
        carried = carried + stream_mixing[:, :, :, source, None] * widened[:, :, None, source, :]
    mixed_rows = carried.astype(jnp.bfloat16)
    return (mixed_rows, (normed, context))

def section_backward(streams, emitted_adjoint, segment_ids, blend_linear_map, rescale_amplitude, attend_entry_maps, attend_exit_map):
    batch_groups, sequence_length = (streams.shape[0], streams.shape[1])
    qkv_hole = jnp.zeros((batch_groups, sequence_length, attend_entry_maps.shape[1]), jnp.bfloat16)
    att_hole = jnp.zeros((batch_groups, sequence_length, attend_exit_map.shape[1]), jnp.float32)

    def local_fn(streams_in, proj_in, gain_in, qkv_in, att_in):
        return stream_layer(streams_in, segment_ids, proj_in, gain_in, attend_entry_maps, attend_exit_map, qkv_in, att_in)
    primal_out, pullback, kept = jax.vjp(local_fn, streams, blend_linear_map, rescale_amplitude, qkv_hole, att_hole, has_aux=True)
    stream_cot, proj_cot, gain_cot, qkv_cot, att_cot = pullback(emitted_adjoint)
    normed, context = kept
    grad_qkv = jnp.dot(normed.reshape(-1, normed.shape[-1]).T, qkv_cot.reshape(-1, qkv_cot.shape[-1]), preferred_element_type=jnp.float32)
    grad_out = jnp.dot(context.reshape(-1, context.shape[-1]).T, att_cot.astype(jnp.bfloat16).reshape(-1, att_cot.shape[-1]), preferred_element_type=jnp.float32)
    return (stream_cot, (grad_qkv, grad_out, proj_cot, gain_cot))

def reference(saved_entering_lanes, opening_adjoint, final_later_adjoint, document_labels, blend_linear_map, rescale_amplitude, attend_entry_maps, attend_exit_map):

    def per_section(items):
        streams, emitted_adjoint, segment_ids, proj_one, gain_one, qkv_one, out_one = items
        shaped = streams.reshape(N_DP, TOK, SKIP_LANES, HIDDEN_WIDTH)
        cot_shaped = emitted_adjoint.reshape(N_DP, TOK, SKIP_LANES, HIDDEN_WIDTH)
        stream_cot, grads = section_backward(shaped, cot_shaped, segment_ids.reshape(N_DP, TOK), proj_one, gain_one, qkv_one, out_one)
        return (stream_cot.reshape(WORDS_PER_STEP, SKIP_LANES, HIDDEN_WIDTH), grads)
    sent_list = []
    totals = None
    earlier_outcome = opening_adjoint
    for tick_idx in range(TICKS):
        if tick_idx == 0:
            emitted_adjoint = opening_adjoint
        else:
            emitted_adjoint = jnp.concatenate([earlier_outcome[1:], final_later_adjoint[tick_idx - 1][None]], axis=0)
        earlier_outcome, grads = lax.map(per_section, (saved_entering_lanes[:, tick_idx], emitted_adjoint, document_labels[:, tick_idx], blend_linear_map, rescale_amplitude, attend_entry_maps, attend_exit_map))
        if tick_idx == 0:
            totals = grads
        else:
            totals = jax.tree.map(jnp.add, totals, grads)
        sent_list.append(earlier_outcome)
    sent = jnp.stack(sent_list, axis=1)
    return (sent, totals[0], totals[1], totals[2], totals[3])
```

```python
import jax
import jax.numpy as jnp
from jax import lax
from jax.experimental import pallas as pl
from jax.experimental.pallas import tpu as pltpu
from jax.sharding import PartitionSpec as P

F32 = jnp.float32
BF16 = jnp.bfloat16
LANES = 4
D = 1024
T = 128
HEADS = 8
PAIRS = HEADS // 2
INNER = 512
SINK = 20
EPS = 1e-6
ROWS = 16
SHARD_ROWS = 288
QKV_TAIL = 128
OUT_AT = 192
PROJ_AT = 256
GAIN_AT = 272
NN = (((1,), (0,)), ((), ()))
NT = (((1,), (1,)), ((), ()))
TN = (((0,), (0,)), ((), ()))


def dot(a, b, dims=NN):
    return lax.dot_general(a, b, dims, preferred_element_type=F32)


def split(value):
    high = value.astype(BF16)
    return high, (value - high.astype(F32)).astype(BF16)


def iota(shape, axis):
    return lax.broadcasted_iota(jnp.int32, shape, axis)


def group_sum(block):
    block = block + pltpu.roll(block, 1, 0)
    return block + pltpu.roll(block, 2, 0)


def doubled(block):
    lower = iota(block.shape, 0) < 4
    turned = pltpu.roll(block, 4, 0)
    return jnp.where(lower, block, turned), jnp.where(lower, turned, block)


def tokens_first(rows):
    short = 128 - rows.shape[0]
    if short:
        rows = jnp.concatenate([rows, jnp.zeros((short, T), F32)], axis=0)
    return rows.T


def head_ones():
    return (iota((128, 128), 0) // 64 == iota((128, 128), 1) // 64).astype(BF16)


def head_mean(value, ones):
    high, low = split(value)
    return (dot(high, ones) + dot(low, ones)) * (1.0 / 64.0)


def half_masks():
    low = iota((1, 128), 1) < 64
    return low, [low.astype(F32).astype(BF16), (~low).astype(F32).astype(BF16)]


def stacked_map(bt_ref, bhl):
    high, low = split(jnp.concatenate([bt_ref[...], jnp.zeros((8, LANES * D), F32)], axis=0))
    bhl[0:32, :] = high
    bhl[32:64, :] = low


def forward(x, bhl, gain, w, wo, seg, s):
    eye = iota((T, T), 0) == iota((T, T), 1)
    raw = jnp.zeros((64, T), F32)
    square = jnp.zeros((T, T), F32)
    for j in range(LANES):
        raw = raw + dot(bhl[:, j * D : (j + 1) * D], x[j], NT)
        square = square + dot(x[j], x[j], NT)
    mean = jnp.sum(jnp.where(eye, square, 0.0), axis=0, keepdims=True) * (1.0 / (LANES * D))
    inv = lax.rsqrt(mean + EPS)
    mc = (raw[0:24] + raw[32:56]) * inv
    s["mc"][...] = jnp.concatenate([mc, jnp.broadcast_to(inv, (8, T))], axis=0)
    lower = iota((8, T), 0) < 4
    gates = jax.nn.sigmoid(mc[0:8])
    gates = jnp.where(lower, gates, 2.0 * gates)
    first = doubled(jnp.exp(mc[8:16]))
    second = doubled(jnp.exp(mc[16:24]))

    def one_round(index, current):
        sums = [1.0 / group_sum(a) for a in current]
        current = [a * b for a, b in zip(current, sums)]
        for i in range(LANES):
            s["sink"][index, i] = current[i]
            s["sink"][index, 4 + i] = sums[i]
        total = 1.0 / ((current[0] + current[1]) + (current[2] + current[3]))
        current = [a * total for a in current]
        for i in range(LANES):
            s["sink"][index, 8 + i] = current[i]
        s["sink"][index, 12] = total
        return tuple(current)

    settled = lax.fori_loop(0, SINK, one_round, first + second)
    s["coef"][...] = tokens_first(
        jnp.concatenate(
            [
                gates,
                jnp.where(lower, settled[0], settled[1]),
                jnp.where(lower, settled[2], settled[3]),
            ],
            axis=0,
        )
    )

    def join_rows(block, _):
        rows = pl.ds(pl.multiple_of(block * ROWS, ROWS), ROWS)
        c = s["coef"][rows, :]
        joined = c[:, 0:1] * x[0, rows, :].astype(F32)
        for i in range(1, LANES):
            joined = joined + c[:, i : i + 1] * x[i, rows, :].astype(F32)
        r = lax.rsqrt(jnp.mean(joined * joined, axis=-1, keepdims=True) + EPS)
        s["joined"][rows, :] = joined
        s["r"][rows, :] = jnp.broadcast_to(r, (ROWS, 128))
        s["normed"][rows, :] = (joined * r * gain[...]).astype(BF16)
        return 0

    lax.fori_loop(0, T // ROWS, join_rows, 0)
    projected = dot(s["normed"][...], w[...]).astype(BF16)
    s["proj"][...] = projected
    ones = head_ones()
    for at in range(2 * PAIRS):
        lanes = slice(at * 128, at * 128 + 128)
        wide = projected[:, lanes].astype(F32)
        scale = lax.rsqrt(head_mean(wide * wide, ones) + EPS)
        s["scale"][:, lanes] = scale
        s["qk"][:, lanes] = (wide * scale).astype(BF16)
    ids = jnp.broadcast_to(seg[...].astype(F32), (T, T))
    allowed = (ids == ids.T) & (iota((T, T), 1) <= iota((T, T), 0))
    low, masks = half_masks()
    for pair in range(PAIRS):
        lanes = slice(pair * 128, pair * 128 + 128)
        q = s["qk"][:, lanes]
        k = s["qk"][:, pl.ds(INNER + pair * 128, 128)]
        v = s["proj"][:, pl.ds(2 * INNER + pair * 128, 128)]
        parts = []
        for half in range(2):
            scores = dot(q * masks[half], k, NT) * 0.125
            free = jnp.where(allowed, jnp.exp(scores), 0.0)
            weights = free / jnp.sum(free, axis=-1, keepdims=True)
            s["weights"][2 * pair + half] = weights
            parts.append(dot(weights.astype(BF16), v))
        s["ctx"][:, lanes] = jnp.where(low, parts[0], parts[1]).astype(BF16)
    s["att"][...] = dot(s["ctx"][...], wo[...]).astype(BF16)


def diagonal(product, eye):
    return jnp.sum(jnp.where(eye, product, 0.0), axis=0, keepdims=True)


def by_sublane(rows):
    at = iota((8, T), 0) % 4
    block = jnp.broadcast_to(rows[3], (8, T))
    for k in range(3):
        block = jnp.where(at == k, jnp.broadcast_to(rows[k], (8, T)), block)
    return block


def backward(x, g, bhl, gain, w, wo, s, o, t):
    eye = iota((T, T), 0) == iota((T, T), 1)

    def att_rows(block, _):
        rows = pl.ds(pl.multiple_of(block * ROWS, ROWS), ROWS)
        c = s["coef"][rows, :]
        total = c[:, 4:5] * g[0, rows, :].astype(F32)
        for i in range(1, LANES):
            total = total + c[:, 4 + i : 5 + i] * g[i, rows, :].astype(F32)
        o["datt"][rows, :] = total.astype(BF16)
        return 0

    lax.fori_loop(0, T // ROWS, att_rows, 0)
    dctx = dot(o["datt"][...], wo[...], NT).astype(BF16)
    low, masks = half_masks()
    ones = head_ones()

    def norm_back(dn, at):
        lanes = pl.ds(at * 128, 128)
        wide = s["proj"][:, lanes].astype(F32)
        scale = s["scale"][:, lanes]
        dn = dn.astype(BF16).astype(F32)
        moment = head_mean(dn * wide, ones)
        o["dproj"][:, lanes] = (scale * (dn - wide * (scale * scale * moment))).astype(BF16)

    for pair in range(PAIRS):
        lanes = slice(pair * 128, pair * 128 + 128)
        q = s["qk"][:, lanes]
        k = s["qk"][:, pl.ds(INNER + pair * 128, 128)]
        v = s["proj"][:, pl.ds(2 * INNER + pair * 128, 128)]
        dc = dctx[:, lanes]
        dq, dk, dv = [], [], []
        for half in range(2):
            weights = s["weights"][2 * pair + half]
            dw = dot(dc * masks[half], v, NT).astype(BF16).astype(F32)
            dscore = weights * (dw - jnp.sum(dw * weights, axis=-1, keepdims=True)) * 0.125
            dq.append(dot(dscore.astype(BF16), k))
            dk.append(dot(dscore.T.astype(BF16), q))
            dv.append(dot(weights.T.astype(BF16), dc))
        o["dproj"][:, pl.ds(2 * INNER + pair * 128, 128)] = jnp.where(low, dv[0], dv[1]).astype(BF16)
        norm_back(jnp.where(low, dq[0], dq[1]), pair)
        norm_back(jnp.where(low, dk[0], dk[1]), PAIRS + pair)
    t["dn"][...] = dot(o["dproj"][...], w[...], NT).astype(BF16)

    def joined_rows(block, total):
        rows = pl.ds(pl.multiple_of(block * ROWS, ROWS), ROWS)
        r = s["r"][rows, 0:1]
        joined = s["joined"][rows, :]
        dn = t["dn"][rows, :].astype(F32)
        total = total + jnp.sum(dn * (joined * r), axis=0, keepdims=True)
        scaled = dn * gain[...]
        moment = jnp.mean(scaled * joined, axis=-1, keepdims=True)
        t["dj"][rows, :] = r * scaled - joined * (r * r * r * moment)
        return total

    o["dgain"][...] = lax.fori_loop(0, T // ROWS, joined_rows, jnp.zeros((1, D), F32))

    dj = t["dj"][...].astype(BF16)
    pre = [diagonal(dot(dj, x[j], NT), eye) for j in range(LANES)]
    post = [diagonal(dot(g[i], s["att"][...], NT), eye) for i in range(LANES)]
    dmix = tuple(
        by_sublane([diagonal(dot(g[i], x[j], NT), eye) for j in range(LANES)])
        for i in range(LANES)
    )

    def one_round(step, current):
        index = SINK - 1 - step
        after = [s["sink"][index, 8 + i] for i in range(LANES)]
        pull = [a * b for a, b in zip(current, after)]
        pull = (pull[0] + pull[1]) + (pull[2] + pull[3])
        total = s["sink"][index, 12]
        current = [(a - pull) * total for a in current]
        between = [s["sink"][index, i] for i in range(LANES)]
        sums = [s["sink"][index, 4 + i] for i in range(LANES)]
        return tuple(
            (a - group_sum(a * b)) * c for a, b, c in zip(current, between, sums)
        )

    dmix = lax.fori_loop(0, SINK, one_round, dmix)
    lower = iota((8, T), 0) < 4
    mc = s["mc"][...]
    inv = mc[24:32]
    gates = jax.nn.sigmoid(mc[0:8])
    dgates = jnp.where(lower, by_sublane(pre), 2.0 * by_sublane(post))
    dmc = [
        dgates * gates * (1.0 - gates),
        jnp.where(lower, dmix[0], dmix[1]) * jnp.exp(mc[8:16]),
        jnp.where(lower, dmix[2], dmix[3]) * jnp.exp(mc[16:24]),
    ]
    dot_mc = dmc[0] * mc[0:8] + dmc[1] * mc[8:16] + dmc[2] * mc[16:24]
    dot_mc = jnp.sum(dot_mc, axis=0, keepdims=True)
    kappa = inv * inv * dot_mc * (1.0 / (LANES * D))
    scaled = jnp.concatenate([a * inv for a in dmc] + [jnp.zeros((8, T), F32)], axis=0)
    back = tokens_first(jnp.concatenate([scaled, scaled, kappa], axis=0))
    t["back"][...] = back
    lead = back[:, 0:64].astype(BF16)
    rows_first = scaled.astype(BF16)
    for j in range(LANES):
        cols = slice(j * D, (j + 1) * D)
        o["dproj_map"][:, cols] = dot(rows_first, x[j])
        t["f"][j] = dot(lead, bhl[:, cols])

    def stream_rows(block, _):
        rows = pl.ds(pl.multiple_of(block * ROWS, ROWS), ROWS)
        c = s["coef"][rows, :]
        kap = t["back"][rows, 64:65]
        dj = t["dj"][rows, :]
        gs = [g[i, rows, :].astype(F32) for i in range(LANES)]
        for j in range(LANES):
            total = t["f"][j, rows, :] + c[:, j : j + 1] * dj - kap * x[j, rows, :].astype(F32)
            for i in range(LANES):
                at = 8 + LANES * i + j
                total = total + c[:, at : at + 1] * gs[i]
            o["dx"][j, rows, :] = total.astype(BF16)
        return 0

    lax.fori_loop(0, T // ROWS, stream_rows, 0)


SAVED = (
    ("mc", (32, T), F32),
    ("sink", (SINK, 13, 8, T), F32),
    ("coef", (T, 128), F32),
    ("joined", (T, D), F32),
    ("r", (T, 128), F32),
    ("normed", (T, D), BF16),
    ("proj", (T, 3 * INNER), BF16),
    ("scale", (T, 2 * INNER), F32),
    ("qk", (T, 2 * INNER), BF16),
    ("weights", (HEADS, T, T), F32),
    ("ctx", (T, INNER), BF16),
    ("att", (T, D), BF16),
)
BACK = (
    ("dx", (LANES, T, D), BF16),
    ("dproj", (T, 3 * INNER), BF16),
    ("datt", (T, D), BF16),
    ("dproj_map", (32, LANES * D), F32),
    ("dgain", (1, D), F32),
)
TEMPS = (
    ("dn", (T, D), BF16),
    ("dj", (T, D), F32),
    ("back", (T, 128), F32),
    ("f", (LANES, T, D), F32),
)
KEPT = ("normed", "ctx")
BHL = (64, LANES * D)


def shapes(table):
    return [jax.ShapeDtypeStruct(shape, dtype) for _, shape, dtype in table]


def scratch(table):
    return [pltpu.VMEM(shape, dtype) for _, shape, dtype in table]


def named(table, refs):
    return {name: ref for (name, _, _), ref in zip(table, refs)}


def call(body, outs, scratches, args, flops, name):
    moved = sum(a.size * a.dtype.itemsize for a in args)
    moved += sum(a.size * a.dtype.itemsize for a in outs)
    whole = pl.BlockSpec(memory_space=pltpu.VMEM)
    return pl.pallas_call(
        body,
        out_shape=outs,
        in_specs=[whole] * len(args),
        out_specs=[whole] * len(outs),
        scratch_shapes=scratches,
        compiler_params=pltpu.CompilerParams(vmem_limit_bytes=56 * 1024 * 1024),
        cost_estimate=pl.CostEstimate(flops=flops, bytes_accessed=moved, transcendentals=0),
        name=name,
    )(*args)


SAVED_IN = [e for e in SAVED if e[0] not in KEPT]
SAVED_OUT = [e for e in SAVED if e[0] in KEPT]


def whole_tick(x, g, seg, bt, gain, w, wo):
    def body(x, g, seg, bt, gain, w, wo, *rest):
        outs = rest[: len(BACK) + len(KEPT)]
        rest = rest[len(outs) :]
        o = named(BACK, outs)
        s = named(SAVED_OUT, outs[len(BACK) :])
        s.update(named(SAVED_IN, rest))
        rest = rest[len(SAVED_IN) :]
        t = named(TEMPS, rest)
        bhl = rest[len(TEMPS)]
        stacked_map(bt, bhl)
        forward(x, bhl, gain, w, wo, seg, s)
        backward(x, g, bhl, gain, w, wo, s, o, t)

    return call(
        body,
        shapes(BACK) + shapes(SAVED_OUT),
        scratch(SAVED_IN) + scratch(TEMPS) + [pltpu.VMEM(BHL, BF16)],
        (x, g, seg, bt, gain, w, wo),
        4_000_000_000,
        "whole_tick",
    )


def forward_tick(x, seg, bt, gain, w, wo):
    def body(x, seg, bt, gain, w, wo, *outs):
        bhl = outs[len(SAVED)]
        stacked_map(bt, bhl)
        forward(x, bhl, gain, w, wo, seg, named(SAVED, outs))

    saved = call(
        body,
        shapes(SAVED) + [jax.ShapeDtypeStruct(BHL, BF16)],
        [],
        (x, seg, bt, gain, w, wo),
        1_000_000_000,
        "forward_tick",
    )
    return saved


def fill_shards(first, second, out, n):
    rows = D // n
    normed = jnp.concatenate([first["normed"][...], second["normed"][...]], axis=0)
    for at in range(6):
        cols = slice(at * 256, at * 256 + 256)
        right = jnp.concatenate([first["dproj"][:, cols], second["dproj"][:, cols]], axis=0)
        product = dot(normed, right, TN).astype(BF16)
        for d in range(n):
            part = product[d * rows : (d + 1) * rows]
            if at < 4:
                out[d, 0:rows, cols] = part
            else:
                left = (at - 4) * 256
                half = rows // 2
                out[d, QKV_TAIL : QKV_TAIL + half, left : left + 256] = part[0:half]
                out[d, QKV_TAIL : QKV_TAIL + half, 512 + left : 768 + left] = part[half:]
    ctx = jnp.concatenate([first["ctx"][...], second["ctx"][...]], axis=0)
    rows = INNER // n
    for at in range(4):
        cols = slice(at * 256, at * 256 + 256)
        right = jnp.concatenate([first["datt"][:, cols], second["datt"][:, cols]], axis=0)
        product = dot(ctx, right, TN).astype(BF16)
        for d in range(n):
            out[d, OUT_AT : OUT_AT + rows, cols] = product[d * rows : (d + 1) * rows]
    for d in range(n):
        cols = slice(d * 512, d * 512 + 512)
        proj = first["dproj_map"][:, cols] + second["dproj_map"][:, cols]
        out[d, PROJ_AT : PROJ_AT + 16, 0:512] = proj[0:16].astype(BF16)
        out[d, PROJ_AT : PROJ_AT + 16, 512:1024] = proj[16:32].astype(BF16)
        gain = first["dgain"][:, d * 128 : d * 128 + 128] + second["dgain"][:, d * 128 : d * 128 + 128]
        out[d, GAIN_AT : GAIN_AT + 16, 0:128] = jnp.broadcast_to(gain, (16, 128)).astype(BF16)
        out[d, GAIN_AT : GAIN_AT + 16, 128:1024] = jnp.zeros((16, 896), BF16)


EARLIER = ("dproj", "datt", "dproj_map", "dgain", "normed", "ctx")


def backward_tick(x, g, gain, w, wo, saved, earlier, n):
    def body(x, g, gain, w, wo, *rest):
        s = named(SAVED, rest)
        bhl = rest[len(SAVED)]
        rest = rest[len(SAVED) + 1 :]
        first = dict(zip(EARLIER, rest))
        rest = rest[len(EARLIER) :]
        o = {"dx": rest[0]}
        out = rest[1]
        rest = rest[2:]
        o.update(named(BACK[1:], rest))
        t = named(TEMPS, rest[len(BACK) - 1 :])
        backward(x, g, bhl, gain, w, wo, s, o, t)
        second = dict(o)
        second["normed"] = s["normed"]
        second["ctx"] = s["ctx"]
        fill_shards(first, second, out, n)

    return call(
        body,
        shapes(BACK[:1]) + [jax.ShapeDtypeStruct((n, SHARD_ROWS, D), BF16)],
        scratch(BACK[1:]) + scratch(TEMPS),
        (x, g, gain, w, wo, *saved, *[earlier[k] for k in EARLIER]),
        4_000_000_000,
        "backward_tick",
    )


def shards(
    saved_entering_lanes,
    opening_adjoint,
    final_later_adjoint,
    document_labels,
    blend_linear_map,
    rescale_amplitude,
    attend_entry_maps,
    attend_exit_map,
):
    n = lax.axis_size("dp")
    layers = lax.axis_size("section")
    last = lax.axis_index("section") == layers - 1
    lanes_first = lambda a: jnp.transpose(a, (1, 0, 2))
    x0 = lanes_first(saved_entering_lanes[0, 0])
    x1 = lanes_first(saved_entering_lanes[0, 1])
    opening = lanes_first(opening_adjoint[0])
    final = lanes_first(final_later_adjoint[0])
    bt = blend_linear_map[0].T
    gain = rescale_amplitude
    w = attend_entry_maps[0]
    wo = attend_exit_map[0]
    outs = whole_tick(x0, opening, document_labels[0, 0:1], bt, gain, w, wo)
    earlier = dict(zip([e[0] for e in BACK] + [e[0] for e in SAVED_OUT], outs))
    dx0 = earlier["dx"]
    received = lax.ppermute(dx0, "section", [(i + 1, i) for i in range(layers - 1)])
    saved = forward_tick(x1, document_labels[0, 1:2], bt, gain, w, wo)
    later = jnp.where(last, final, received)
    dx1, terms = backward_tick(x1, later, gain, w, wo, saved, earlier, n)
    mine = lax.psum_scatter(terms, "dp", scatter_dimension=0, tiled=False)
    sent = jnp.stack([jnp.transpose(dx0, (1, 0, 2)), jnp.transpose(dx1, (1, 0, 2))])[None]
    mine = mine.astype(F32)
    rows = D // n
    half = rows // 2
    tail = mine[QKV_TAIL : QKV_TAIL + half]
    tail = jnp.concatenate([tail[:, :512], tail[:, 512:]], axis=0)
    grad_qkv = jnp.concatenate([mine[:rows], tail], axis=1)
    grad_out = mine[OUT_AT : OUT_AT + INNER // n]
    proj = jnp.concatenate(
        [mine[PROJ_AT : PROJ_AT + 16, :512], mine[PROJ_AT : PROJ_AT + 8, 512:]], axis=0
    )
    return (
        sent,
        grad_qkv[None],
        grad_out[None],
        proj.T[None],
        mine[GAIN_AT : GAIN_AT + 1, :rows],
    )


def solution(mesh):
    return jax.shard_map(
        shards,
        mesh=mesh,
        in_specs=(
            P("section", None, "dp", None, None),
            P("section", "dp", None, None),
            P(None, "dp", None, None),
            P("section", None, "dp"),
            P("section", None, None),
            P("section", None),
            P("section", None, None),
            P("section", None, None),
        ),
        out_specs=(
            P("section", None, "dp", None, None),
            P("section", "dp", None),
            P("section", "dp", None),
            P("section", "dp", None),
            P("section", "dp"),
        ),
        check_vma=False,
    )
```

```python
import functools

import jax
import jax.numpy as jnp
from jax import lax
from jax.experimental import pallas as pl
from jax.experimental.pallas import tpu as pltpu
from jax.sharding import PartitionSpec as P

F32 = jnp.float32
BF16 = jnp.bfloat16
LANES = 4
D = 1024
T = 128
HEADS = 8
PAIRS = HEADS // 2
INNER = 512
SINK = 20
EPS = 1e-6
ROWS = 16
RUN = 4
FORWARD_COST = 1
FINISH_COST = 100
RIGHT = 3 * INNER + D
LEFT = D + INNER
FRONT = 80
NN = (((1,), (0,)), ((), ()))
NT = (((1,), (1,)), ((), ()))
TN = (((0,), (0,)), ((), ()))


def dot(a, b, dims=NN):
    return lax.dot_general(a, b, dims, preferred_element_type=F32)


def split(value):
    high = value.astype(BF16)
    return high, (value - high.astype(F32)).astype(BF16)


def iota(shape, axis):
    return lax.broadcasted_iota(jnp.int32, shape, axis)


def group_sum(block):
    block = block + pltpu.roll(block, 1, 0)
    return block + pltpu.roll(block, 2, 0)


def doubled(block):
    lower = iota(block.shape, 0) < 4
    turned = pltpu.roll(block, 4, 0)
    return jnp.where(lower, block, turned), jnp.where(lower, turned, block)


def tokens_first(rows):
    short = 128 - rows.shape[0]
    if short:
        rows = jnp.concatenate([rows, jnp.zeros((short, T), F32)], axis=0)
    return rows.T


def head_ones():
    return (iota((128, 128), 0) // 64 == iota((128, 128), 1) // 64).astype(BF16)


def head_mean(value, ones):
    high, low = split(value)
    return (dot(high, ones) + dot(low, ones)) * (1.0 / 64.0)


def half_masks():
    low = iota((1, 128), 1) < 64
    return low, [low.astype(F32).astype(BF16), (~low).astype(F32).astype(BF16)]


def stacked_map(bt_ref, bhl):
    high, low = split(jnp.concatenate([bt_ref[...], jnp.zeros((8, LANES * D), F32)], axis=0))
    bhl[0:32, :] = high
    bhl[32:64, :] = low


def forward(x, bhl, gain, w, wo, seg, s):
    eye = iota((T, T), 0) == iota((T, T), 1)
    raw = jnp.zeros((64, T), F32)
    square = jnp.zeros((T, T), F32)
    for j in range(LANES):
        raw = raw + dot(bhl[:, j * D : (j + 1) * D], x[j], NT)
        square = square + dot(x[j], x[j], NT)
    mean = jnp.sum(jnp.where(eye, square, 0.0), axis=0, keepdims=True) * (1.0 / (LANES * D))
    inv = lax.rsqrt(mean + EPS)
    mc = (raw[0:24] + raw[32:56]) * inv
    s["mc"][...] = jnp.concatenate([mc, jnp.broadcast_to(inv, (8, T))], axis=0)
    lower = iota((8, T), 0) < 4
    gates = jax.nn.sigmoid(mc[0:8])
    gates = jnp.where(lower, gates, 2.0 * gates)
    first = doubled(jnp.exp(mc[8:16]))
    second = doubled(jnp.exp(mc[16:24]))

    def one_round(index, current):
        sums = [1.0 / group_sum(a) for a in current]
        current = [a * b for a, b in zip(current, sums)]
        for i in range(LANES):
            s["sink"][index, i] = current[i]
            s["sink"][index, 4 + i] = sums[i]
        total = 1.0 / ((current[0] + current[1]) + (current[2] + current[3]))
        current = [a * total for a in current]
        for i in range(LANES):
            s["sink"][index, 8 + i] = current[i]
        s["sink"][index, 12] = total
        return tuple(current)

    settled = lax.fori_loop(0, SINK, one_round, first + second)
    s["coef"][...] = tokens_first(
        jnp.concatenate(
            [
                gates,
                jnp.where(lower, settled[0], settled[1]),
                jnp.where(lower, settled[2], settled[3]),
            ],
            axis=0,
        )
    )

    def join_rows(block, _):
        rows = pl.ds(pl.multiple_of(block * ROWS, ROWS), ROWS)
        c = s["coef"][rows, :]
        joined = c[:, 0:1] * x[0, rows, :].astype(F32)
        for i in range(1, LANES):
            joined = joined + c[:, i : i + 1] * x[i, rows, :].astype(F32)
        r = lax.rsqrt(jnp.mean(joined * joined, axis=-1, keepdims=True) + EPS)
        s["joined"][rows, :] = joined
        s["r"][rows, :] = jnp.broadcast_to(r, (ROWS, 128))
        s["normed"][rows, :] = (joined * r * gain[...]).astype(BF16)
        return 0

    lax.fori_loop(0, T // ROWS, join_rows, 0)
    projected = dot(s["normed"][...], w[...]).astype(BF16)
    s["proj"][...] = projected
    ones = head_ones()
    for at in range(2 * PAIRS):
        lanes = slice(at * 128, at * 128 + 128)
        wide = projected[:, lanes].astype(F32)
        scale = lax.rsqrt(head_mean(wide * wide, ones) + EPS)
        s["scale"][:, lanes] = scale
        s["qk"][:, lanes] = (wide * scale).astype(BF16)
    ids = jnp.broadcast_to(seg[...].astype(F32), (T, T))
    allowed = (ids == ids.T) & (iota((T, T), 1) <= iota((T, T), 0))
    low, masks = half_masks()
    for pair in range(PAIRS):
        lanes = slice(pair * 128, pair * 128 + 128)
        q = s["qk"][:, lanes]
        k = s["qk"][:, pl.ds(INNER + pair * 128, 128)]
        v = s["proj"][:, pl.ds(2 * INNER + pair * 128, 128)]
        parts = []
        for half in range(2):
            scores = dot(q * masks[half], k, NT) * 0.125
            free = jnp.where(allowed, jnp.exp(scores), 0.0)
            weights = free / jnp.sum(free, axis=-1, keepdims=True)
            s["weights"][2 * pair + half] = weights
            parts.append(dot(weights.astype(BF16), v))
        s["ctx"][:, lanes] = jnp.where(low, parts[0], parts[1]).astype(BF16)
    s["att"][...] = dot(s["ctx"][...], wo[...]).astype(BF16)


def diagonal(product, eye):
    return jnp.sum(jnp.where(eye, product, 0.0), axis=0, keepdims=True)


def by_sublane(rows):
    at = iota((8, T), 0) % 4
    block = jnp.broadcast_to(rows[3], (8, T))
    for k in range(3):
        block = jnp.where(at == k, jnp.broadcast_to(rows[k], (8, T)), block)
    return block


def adjoint_rows(g, s, out):
    def att_rows(block, _):
        rows = pl.ds(pl.multiple_of(block * ROWS, ROWS), ROWS)
        c = s["coef"][rows, :]
        total = c[:, 4:5] * g[0, rows, :].astype(F32)
        for i in range(1, LANES):
            total = total + c[:, 4 + i : 5 + i] * g[i, rows, :].astype(F32)
        out[rows, :] = total.astype(BF16)
        return 0

    lax.fori_loop(0, T // ROWS, att_rows, 0)


def attention_back(datt, wo, s, out):
    dctx = dot(datt[...], wo[...], NT).astype(BF16)
    low, masks = half_masks()
    ones = head_ones()

    def norm_back(dn, at):
        lanes = pl.ds(at * 128, 128)
        wide = s["proj"][:, lanes].astype(F32)
        scale = s["scale"][:, lanes]
        dn = dn.astype(BF16).astype(F32)
        moment = head_mean(dn * wide, ones)
        out[:, lanes] = (scale * (dn - wide * (scale * scale * moment))).astype(BF16)

    for pair in range(PAIRS):
        lanes = slice(pair * 128, pair * 128 + 128)
        q = s["qk"][:, pl.ds(pair * 128, 128)]
        key = s["qk"][:, pl.ds(INNER + pair * 128, 128)]
        v = s["proj"][:, pl.ds(2 * INNER + pair * 128, 128)]
        dc = dctx[:, lanes]
        dq, dk, dv = [], [], []
        for side in range(2):
            weights = s["weights"][2 * pair + side]
            dw = dot(dc * masks[side], v, NT).astype(BF16).astype(F32)
            dscore = weights * (dw - jnp.sum(dw * weights, axis=-1, keepdims=True)) * 0.125
            dq.append(dot(dscore.astype(BF16), key))
            dk.append(dot(dscore.T.astype(BF16), q))
            dv.append(dot(weights.T.astype(BF16), dc))
        out[:, pl.ds(2 * INNER + pair * 128, 128)] = jnp.where(low, dv[0], dv[1]).astype(BF16)
        norm_back(jnp.where(low, dq[0], dq[1]), pair)
        norm_back(jnp.where(low, dk[0], dk[1]), PAIRS + pair)


def stream_back(x, g, bhl, gain, w, s, o, t, put):
    eye = iota((T, T), 0) == iota((T, T), 1)
    t["dn"][...] = dot(o["dproj"][...], w[...], NT).astype(BF16)

    def joined_rows(block, total):
        rows = pl.ds(pl.multiple_of(block * ROWS, ROWS), ROWS)
        r = s["r"][rows, 0:1]
        joined = s["joined"][rows, :]
        dn = t["dn"][rows, :].astype(F32)
        total = total + jnp.sum(dn * (joined * r), axis=0, keepdims=True)
        scaled = dn * gain[...]
        moment = jnp.mean(scaled * joined, axis=-1, keepdims=True)
        t["dj"][rows, :] = r * scaled - joined * (r * r * r * moment)
        return total

    o["dgain"][...] = lax.fori_loop(0, T // ROWS, joined_rows, jnp.zeros((1, D), F32))

    dj = t["dj"][...].astype(BF16)
    pre = [diagonal(dot(dj, x[j], NT), eye) for j in range(LANES)]
    post = [diagonal(dot(g[i], s["att"][...], NT), eye) for i in range(LANES)]
    dmix = tuple(
        by_sublane([diagonal(dot(g[i], x[j], NT), eye) for j in range(LANES)])
        for i in range(LANES)
    )

    def one_round(step, current):
        index = SINK - 1 - step
        after = [s["sink"][index, 8 + i] for i in range(LANES)]
        pull = [a * b for a, b in zip(current, after)]
        pull = (pull[0] + pull[1]) + (pull[2] + pull[3])
        total = s["sink"][index, 12]
        current = [(a - pull) * total for a in current]
        between = [s["sink"][index, i] for i in range(LANES)]
        sums = [s["sink"][index, 4 + i] for i in range(LANES)]
        return tuple(
            (a - group_sum(a * b)) * c for a, b, c in zip(current, between, sums)
        )

    dmix = lax.fori_loop(0, SINK, one_round, dmix)
    lower = iota((8, T), 0) < 4
    mc = s["mc"][...]
    inv = mc[24:32]
    gates = jax.nn.sigmoid(mc[0:8])
    dgates = jnp.where(lower, by_sublane(pre), 2.0 * by_sublane(post))
    dmc = [
        dgates * gates * (1.0 - gates),
        jnp.where(lower, dmix[0], dmix[1]) * jnp.exp(mc[8:16]),
        jnp.where(lower, dmix[2], dmix[3]) * jnp.exp(mc[16:24]),
    ]
    dot_mc = dmc[0] * mc[0:8] + dmc[1] * mc[8:16] + dmc[2] * mc[16:24]
    dot_mc = jnp.sum(dot_mc, axis=0, keepdims=True)
    kappa = inv * inv * dot_mc * (1.0 / (LANES * D))
    scaled = jnp.concatenate([a * inv for a in dmc] + [jnp.zeros((8, T), F32)], axis=0)
    back = tokens_first(jnp.concatenate([scaled, scaled, kappa], axis=0))
    t["back"][...] = back
    lead = back[:, 0:64].astype(BF16)
    rows_first = scaled.astype(BF16)
    for j in range(LANES):
        cols = slice(j * D, (j + 1) * D)
        o["dproj_map"][:, cols] = dot(rows_first, x[j])
        t["f"][j] = dot(lead, bhl[:, cols])

    def stream_rows(put, block, _):
        rows = pl.ds(pl.multiple_of(block * ROWS, ROWS), ROWS)
        c = s["coef"][rows, :]
        kap = t["back"][rows, 64:65]
        dj = t["dj"][rows, :]
        gs = [g[i, rows, :].astype(F32) for i in range(LANES)]
        for j in range(LANES):
            total = t["f"][j, rows, :] + c[:, j : j + 1] * dj - kap * x[j, rows, :].astype(F32)
            for i in range(LANES):
                at = 8 + LANES * i + j
                total = total + c[:, at : at + 1] * gs[i]
            put(block, j, total.astype(BF16))
        return 0

    for first, last, place in put:
        lax.fori_loop(first, last, functools.partial(stream_rows, place), 0)


SAVED = (
    ("mc", (32, T), F32),
    ("sink", (SINK, 13, 8, T), F32),
    ("coef", (T, 128), F32),
    ("joined", (T, D), F32),
    ("r", (T, 128), F32),
    ("proj", (T, 3 * INNER), BF16),
    ("scale", (T, 2 * INNER), F32),
    ("qk", (T, 2 * INNER), BF16),
    ("weights", (HEADS, T, T), F32),
    ("att", (T, D), BF16),
    ("bhl", (64, LANES * D), BF16),
)
LEFT_OUT = (("left", (T, LEFT), BF16),)
MAP = (("dproj_map", (32, LANES * D), F32), ("dgain", (1, D), F32))
TEMPS = (
    ("dn", (T, D), BF16),
    ("dj", (T, D), F32),
    ("back", (T, 128), F32),
    ("f", (LANES, T, D), F32),
)
STREAMS = (("g", (LANES, T, D), BF16),)
VMEM = pl.BlockSpec(memory_space=pltpu.VMEM)
ANY = pl.BlockSpec(memory_space=pl.ANY)
SMEM = pl.BlockSpec(memory_space=pltpu.SMEM)


def struct(shape, dtype):
    return jax.ShapeDtypeStruct(shape, dtype)


def shapes(table):
    return [struct(shape, dtype) for _, shape, dtype in table]


def scratch(table):
    return [pltpu.VMEM(shape, dtype) for _, shape, dtype in table]


def names(table):
    return [name for name, _, _ in table]


def named(table, refs):
    return dict(zip(names(table), refs))


def call(body, outs, scratches, args, micros, name, specs=None):
    return pl.pallas_call(
        body,
        out_shape=outs,
        in_specs=specs or [VMEM] * len(args),
        out_specs=[VMEM] * len(outs),
        scratch_shapes=scratches,
        compiler_params=pltpu.CompilerParams(vmem_limit_bytes=56 * 1024 * 1024),
        cost_estimate=pl.CostEstimate(
            flops=micros * 1_000_000_000, bytes_accessed=micros * 2_000_000, transcendentals=0
        ),
        name=name,
    )(*args)


def factors(refs, right, left):
    if right is not None:
        refs["dproj"] = right.at[:, pl.ds(0, 3 * INNER)]
        refs["datt"] = right.at[:, pl.ds(3 * INNER, D)]
    if left is not None:
        refs["normed"] = left.at[:, pl.ds(0, D)]
        refs["ctx"] = left.at[:, pl.ds(D, INNER)]
    return refs


def whole_tick(x, g, seg, bt, gain, w, wo):
    outs = [
        ("dx_front", (LANES, FRONT, D), BF16),
        ("dx_back", (LANES, T - FRONT, D), BF16),
        ("factors", (T, RIGHT + LEFT), BF16),
        *MAP,
    ]

    def body(x, g, seg, bt, gain, w, wo, *rest):
        o = named(outs, rest)
        right = o["factors"].at[:, pl.ds(0, RIGHT)]
        s = factors({}, None, o["factors"].at[:, pl.ds(RIGHT, LEFT)])
        factors(o, right, None)
        rest = rest[len(outs) :]
        s.update(named(SAVED, rest))
        t = named(TEMPS, rest[len(SAVED) :])
        stacked_map(bt, s["bhl"])
        forward(x, s["bhl"], gain, w, wo, seg, s)
        adjoint_rows(g, s, o["datt"])
        attention_back(o["datt"], wo, s, o["dproj"])

        def put_front(block, j, value):
            o["dx_front"][j, pl.ds(pl.multiple_of(block * ROWS, ROWS), ROWS), :] = value

        def put_back(block, j, value):
            at = pl.multiple_of(block * ROWS - FRONT, ROWS)
            o["dx_back"][j, pl.ds(at, ROWS), :] = value

        cut = FRONT // ROWS
        put = ((0, cut, put_front), (cut, T // ROWS, put_back))
        stream_back(x, g, s["bhl"], gain, w, s, o, t, put)

    got = call(
        body,
        shapes(outs),
        scratch(SAVED) + scratch(TEMPS),
        (x, g, seg, bt, gain, w, wo),
        20,
        "whole_tick",
    )
    return named(outs, got)


def forward_tick(x, seg, bt, gain, w, wo):
    table = SAVED + LEFT_OUT

    def body(x, seg, bt, gain, w, wo, *outs):
        s = named(table, outs)
        factors(s, None, s["left"])
        stacked_map(bt, s["bhl"])
        forward(x, s["bhl"], gain, w, wo, seg, s)

    got = call(body, shapes(table), [], (x, seg, bt, gain, w, wo), FORWARD_COST, "forward_tick")
    return named(table, got)


ATTENTION = [e for e in SAVED if e[0] in ("coef", "proj", "scale", "qk", "weights")]


def attention_tick(where, near, far, final, wo, saved, after):
    def body(where, near0, near1, far0, far1, final, after, wo, *rest):
        s = named(ATTENTION, rest)
        g, right, sem = rest[len(ATTENTION) :]

        def fetch(sources):
            copies = [pltpu.make_async_copy(a, b, sem.at[k]) for k, (a, b) in enumerate(sources)]
            for copy in copies:
                copy.start()
            for copy in copies:
                copy.wait()

        head = g.at[:, pl.ds(0, FRONT), :]
        tail = g.at[:, pl.ds(FRONT, T - FRONT), :]

        @pl.when(where[0] == 0)
        def _():
            fetch([(near0, head), (near1, tail)])

        @pl.when(where[0] == 1)
        def _():
            fetch([(far0, head), (far1, tail)])

        @pl.when(where[0] == 2)
        def _():
            fetch([(final, g)])

        o = factors({}, right, None)
        adjoint_rows(g, s, o["datt"])
        attention_back(o["datt"], wo, s, o["dproj"])

    args = (where, *near, *far, final, after, wo, *[saved[k] for k in names(ATTENTION)])
    return call(
        body,
        shapes(STREAMS) + [struct((T, RIGHT), BF16)],
        [pltpu.SemaphoreType.DMA((2,))],
        args,
        5,
        "attention_tick",
        [SMEM] + [ANY] * 6 + [VMEM] * (1 + len(ATTENTION)),
    )


REST = [e for e in SAVED if e[0] in ("mc", "sink", "coef", "joined", "r", "att", "bhl")]


def stream_tick(x, g, gain, w, right, saved, earlier, n, after):
    def body(after, x, g, gain, w, right, *rest):
        s = named(REST, rest)
        rest = rest[len(REST) :]
        first = named(MAP, rest)
        dx, parts, *rest = rest[len(MAP) :]
        o = named(MAP, rest)
        factors(o, right, None)
        t = named(TEMPS, rest[len(MAP) :])

        def put_rows(block, j, value):
            dx[j, pl.ds(pl.multiple_of(block * ROWS, ROWS), ROWS), :] = value

        put = ((0, T // ROWS, put_rows),)
        stream_back(x, g, s["bhl"], gain, w, s, o, t, put)
        width = LANES * D // n
        for d in range(n):
            cols = slice(d * width, d * width + width)
            proj = first["dproj_map"][:, cols] + o["dproj_map"][:, cols]
            lanes = slice(d * (D // n), (d + 1) * (D // n))
            total = first["dgain"][:, lanes] + o["dgain"][:, lanes]
            total = jnp.concatenate([total, jnp.zeros((1, width - D // n), F32)], axis=1)
            total = jnp.broadcast_to(total, (8, width))
            parts[d] = jnp.concatenate([proj[0:24], total], axis=0).astype(BF16)

    return call(
        body,
        [struct((LANES, T, D), BF16), struct((n, 32, LANES * D // n), BF16)],
        scratch(MAP) + scratch(TEMPS),
        (
            after,
            x,
            g,
            gain,
            w,
            right,
            *[saved[k] for k in names(REST)],
            *[earlier[k] for k in names(MAP)],
        ),
        9,
        "stream_tick",
        [ANY] + [VMEM] * (5 + len(REST) + len(MAP)),
    )


STEPS = 4


def turned_factors(place, first, second):
    rows, few = D // (2 * STEPS), INNER // (2 * STEPS)

    def body(place, *refs):
        refs, (left, small) = refs[:STEPS], refs[STEPS:]
        sides = [refs[k].at[:, pl.ds(RIGHT if k % 2 == 0 else 0, LEFT)] for k in range(STEPS)]
        sides = [factors({}, None, side) for side in sides]
        even = place[STEPS] == 0
        for step in range(STEPS):
            chip = place[step]
            at = pl.multiple_of((2 * chip + place[STEPS]) * rows, rows)
            near = pl.multiple_of(chip * rows, rows)
            for k, side in enumerate(sides):
                tokens = slice(k * T, k * T + T)
                block = side["normed"][:, pl.ds(at, rows)].astype(F32).T
                left[step * rows : (step + 1) * rows, tokens] = block.astype(BF16)
                block = side["ctx"][:, pl.ds(near, rows)].astype(F32).T
                block = jnp.where(even, block[0:few], block[few:rows])
                small[step * few : (step + 1) * few, tokens] = block.astype(BF16)

    return call(
        body,
        [struct((STEPS * rows, STEPS * T), BF16), struct((STEPS * few, STEPS * T), BF16)],
        [],
        (place, first[0], second[0], first[1], second[1]),
        FORWARD_COST,
        "turned_factors",
        [SMEM] + [VMEM] * STEPS,
    )


PACKED = 3 * INNER + D // 2


def terms(left, small, rights):
    rows, few = D // (2 * STEPS), INNER // (2 * STEPS)

    def body(left, small, *refs):
        rights, outs = refs[:STEPS], refs[STEPS:]

        def right(at):
            return jnp.concatenate([r[:, at : at + 256] for r in rights], axis=0)

        for at in range(0, 3 * INNER, 256):
            product = dot(left[...], right(at))
            for step in range(STEPS):
                part = product[step * rows : (step + 1) * rows]
                outs[step][:, at : at + 256] = part.astype(outs[step].dtype)
        for at in range(0, D, 256):
            product = dot(small[...], right(3 * INNER + at))
            top = few * (at // (D // 2))
            cols = 3 * INNER + at % (D // 2)
            for step in range(STEPS):
                part = product[step * few : (step + 1) * few]
                outs[step][top : top + few, cols : cols + 256] = part.astype(outs[step].dtype)

    own, *sends = call(
        body,
        [struct((rows, PACKED), F32)] + [struct((rows, PACKED), BF16)] * (STEPS - 1),
        [],
        (left, small, *rights),
        4,
        "terms",
    )
    return own, sends


def finish_terms(terms):
    few = INNER // (2 * STEPS)

    def body(*refs):
        *others, grad_qkv, grad_out = refs[1:]
        total = refs[0][...]
        for other in others:
            total = total + other[...].astype(F32)
        grad_qkv[...] = total[:, : 3 * INNER]
        grad_out[:, : D // 2] = total[:few, 3 * INNER :]
        grad_out[:, D // 2 :] = total[few:, 3 * INNER :]

    rows = terms[0].shape[0]
    outs = [struct((rows, 3 * INNER), F32), struct((few, D), F32)]
    return call(body, outs, [], terms, FINISH_COST, "finish_terms")


def finish_map(parts, n, after):
    width = LANES * D // n

    def body(parts, after, grad_map, grad_gain):
        total = parts[0].astype(F32)
        for d in range(1, n):
            total = total + parts[d].astype(F32)
        grad_map[...] = total[0:24]
        grad_gain[...] = total[24:25, 0 : D // n]

    return call(
        body,
        [struct((24, width), F32), struct((1, D // n), F32)],
        [],
        (parts, after),
        1,
        "finish_map",
        [VMEM, ANY],
    )


def shards(
    saved_entering_lanes,
    opening_adjoint,
    final_later_adjoint,
    document_labels,
    blend_linear_map,
    rescale_amplitude,
    attend_entry_maps,
    attend_exit_map,
):
    n = lax.axis_size("dp")
    layers = lax.axis_size("section")
    section = lax.axis_index("section")
    replica = lax.axis_index("dp")
    chip, core = replica // 2, replica % 2
    lanes_first = lambda a: jnp.transpose(a, (1, 0, 2))
    x0 = lanes_first(saved_entering_lanes[0, 0])
    x1 = lanes_first(saved_entering_lanes[0, 1])
    opening = lanes_first(opening_adjoint[0])
    final = lanes_first(final_later_adjoint[0])
    bt = blend_linear_map[0].T
    gain = rescale_amplitude
    w = attend_entry_maps[0]
    wo = attend_exit_map[0]

    def swap_cores(value):
        return lax.ppermute(value, "dp", [(i, i ^ 1) for i in range(n)])

    def along(value, *chips):
        route = [(2 * a + c, 2 * b + c) for a, b in chips for c in range(2)]
        return lax.ppermute(value, "dp", route)

    first = whole_tick(x0, opening, document_labels[0, 0:1], bt, gain, w, wo)

    near = [(s, s - 1) for s in range(1, layers) if s % RUN]
    cross = range(RUN, layers, RUN)
    hop = lax.ppermute(first["dx_back"], "section", near + [(s, s + RUN - 1) for s in cross])
    front_far = lax.ppermute(first["dx_front"], "section", [(s, s - 1) for s in cross])
    other = swap_cores(first["factors"])
    saved = forward_tick(x1, document_labels[0, 1:2], bt, gain, w, wo)
    coming, later, _ = lax.optimization_barrier((hop, first["dx_front"], saved["coef"]))
    far = lax.ppermute(coming, "section", [(s + RUN - 1, s - 1) for s in cross])
    front_near = lax.ppermute(later, "section", near)
    place = jnp.stack([chip ^ step for step in range(STEPS)] + [core])
    left, small = turned_factors(
        place, (first["factors"], other), (saved["left"], swap_cores(saved["left"]))
    )
    where = jnp.where(section == layers - 1, 2, jnp.where(section % RUN == RUN - 1, 1, 0))
    g, right = attention_tick(
        where[None], (front_near, hop), (front_far, far), final, wo, saved, left
    )
    own, sends = terms(left, small, [first["factors"], right, other, swap_cores(right)])
    by_way = along(sends[2], (0, 1), (3, 2))
    middle = along(sends[2], (1, 2), (2, 1))
    beside = along(sends[0], (0, 1), (1, 0), (2, 3), (3, 2))
    outer = along(sends[1], (0, 2), (3, 1))
    dx1, parts = stream_tick(x1, g, gain, w, right, saved, first, n, own)
    by_way, dx1, parts = lax.optimization_barrier((by_way, dx1, parts))
    both = (sends[1].astype(F32) + by_way.astype(F32)).astype(BF16)
    grads = [own, middle, beside, outer, along(both, (1, 3), (2, 0))]
    parts = lax.all_to_all(parts, "dp", 0, 0)
    grad_qkv, grad_out = finish_terms(grads)
    grad_map, grad_gain = finish_map(parts, n, grad_qkv)
    dx0 = jnp.concatenate([first["dx_front"], first["dx_back"]], axis=1)
    sent = jnp.stack([jnp.transpose(dx0, (1, 0, 2)), jnp.transpose(dx1, (1, 0, 2))])[None]
    return (sent, grad_qkv[None], grad_out[None], grad_map.T[None], grad_gain)


def solution(mesh):
    return jax.shard_map(
        shards,
        mesh=mesh,
        in_specs=(
            P("section", None, "dp", None, None),
            P("section", "dp", None, None),
            P(None, "dp", None, None),
            P("section", None, "dp"),
            P("section", None, None),
            P("section", None),
            P("section", None, None),
            P("section", None, None),
        ),
        out_specs=(
            P("section", None, "dp", None, None),
            P("section", "dp", None),
            P("section", "dp", None),
            P("section", "dp", None),
            P("section", "dp"),
        ),
        check_vma=False,
    )
```

```python
import functools

import jax
import jax.numpy as jnp
from jax import lax
from jax.experimental import pallas as pl
from jax.experimental.pallas import tpu as pltpu
from jax.sharding import PartitionSpec as P

F32 = jnp.float32
BF16 = jnp.bfloat16
LANES = 4
D = 1024
T = 128
HEADS = 8
PAIRS = HEADS // 2
INNER = 512
SINK = 20
EPS = 1e-6
ROWS = 16
RUN = 4
FORWARD_COST = 1
RIGHT = 3 * INNER + D
LEFT = D + INNER
FRONT = 80
NN = (((1,), (0,)), ((), ()))
NT = (((1,), (1,)), ((), ()))
TN = (((0,), (0,)), ((), ()))


def dot(a, b, dims=NN):
    return lax.dot_general(a, b, dims, preferred_element_type=F32)


def split(value):
    high = value.astype(BF16)
    return high, (value - high.astype(F32)).astype(BF16)


def iota(shape, axis):
    return lax.broadcasted_iota(jnp.int32, shape, axis)


def group_sum(block):
    block = block + pltpu.roll(block, 1, 0)
    return block + pltpu.roll(block, 2, 0)


def doubled(block):
    lower = iota(block.shape, 0) < 4
    turned = pltpu.roll(block, 4, 0)
    return jnp.where(lower, block, turned), jnp.where(lower, turned, block)


def tokens_first(rows):
    short = 128 - rows.shape[0]
    if short:
        rows = jnp.concatenate([rows, jnp.zeros((short, T), F32)], axis=0)
    return rows.T


def head_ones():
    return (iota((128, 128), 0) // 64 == iota((128, 128), 1) // 64).astype(BF16)


def head_mean(value, ones):
    high, low = split(value)
    return (dot(high, ones) + dot(low, ones)) * (1.0 / 64.0)


def half_masks():
    low = iota((1, 128), 1) < 64
    return low, [low.astype(F32).astype(BF16), (~low).astype(F32).astype(BF16)]


def stacked_map(bt_ref, bhl):
    high, low = split(jnp.concatenate([bt_ref[...], jnp.zeros((8, LANES * D), F32)], axis=0))
    bhl[0:32, :] = high
    bhl[32:64, :] = low


def forward(x, bhl, gain, w, wo, seg, s, wait):
    eye = iota((T, T), 0) == iota((T, T), 1)
    raw = jnp.zeros((64, T), F32)
    square = jnp.zeros((T, T), F32)
    for j in range(LANES):
        raw = raw + dot(bhl[:, j * D : (j + 1) * D], x[j], NT)
        square = square + dot(x[j], x[j], NT)
    mean = jnp.sum(jnp.where(eye, square, 0.0), axis=0, keepdims=True) * (1.0 / (LANES * D))
    inv = lax.rsqrt(mean + EPS)
    mc = (raw[0:24] + raw[32:56]) * inv
    s["mc"][...] = jnp.concatenate([mc, jnp.broadcast_to(inv, (8, T))], axis=0)
    lower = iota((8, T), 0) < 4
    gates = jax.nn.sigmoid(mc[0:8])
    gates = jnp.where(lower, gates, 2.0 * gates)
    first = doubled(jnp.exp(mc[8:16]))
    second = doubled(jnp.exp(mc[16:24]))

    def one_round(index, current):
        sums = [1.0 / group_sum(a) for a in current]
        current = [a * b for a, b in zip(current, sums)]
        for i in range(LANES):
            s["sink"][index, i] = current[i]
            s["sink"][index, 4 + i] = sums[i]
        total = 1.0 / ((current[0] + current[1]) + (current[2] + current[3]))
        current = [a * total for a in current]
        for i in range(LANES):
            s["sink"][index, 8 + i] = current[i]
        s["sink"][index, 12] = total
        return tuple(current)

    settled = lax.fori_loop(0, SINK, one_round, first + second)
    s["coef"][...] = tokens_first(
        jnp.concatenate(
            [
                gates,
                jnp.where(lower, settled[0], settled[1]),
                jnp.where(lower, settled[2], settled[3]),
            ],
            axis=0,
        )
    )

    def join_rows(block, _):
        rows = pl.ds(pl.multiple_of(block * ROWS, ROWS), ROWS)
        c = s["coef"][rows, :]
        joined = c[:, 0:1] * x[0, rows, :].astype(F32)
        for i in range(1, LANES):
            joined = joined + c[:, i : i + 1] * x[i, rows, :].astype(F32)
        r = lax.rsqrt(jnp.mean(joined * joined, axis=-1, keepdims=True) + EPS)
        s["joined"][rows, :] = joined
        s["r"][rows, :] = jnp.broadcast_to(r, (ROWS, 128))
        s["normed"][rows, :] = (joined * r * gain[...]).astype(BF16)
        return 0

    lax.fori_loop(0, T // ROWS, join_rows, 0)
    wait("w")
    projected = dot(s["normed"][...], w[...]).astype(BF16)
    s["proj"][...] = projected
    ones = head_ones()
    for at in range(2 * PAIRS):
        lanes = slice(at * 128, at * 128 + 128)
        wide = projected[:, lanes].astype(F32)
        scale = lax.rsqrt(head_mean(wide * wide, ones) + EPS)
        s["scale"][:, lanes] = scale
        s["qk"][:, lanes] = (wide * scale).astype(BF16)
    ids = jnp.broadcast_to(seg[...].astype(F32), (T, T))
    allowed = (ids == ids.T) & (iota((T, T), 1) <= iota((T, T), 0))
    low, masks = half_masks()
    for pair in range(PAIRS):
        lanes = slice(pair * 128, pair * 128 + 128)
        q = s["qk"][:, lanes]
        k = s["qk"][:, pl.ds(INNER + pair * 128, 128)]
        v = s["proj"][:, pl.ds(2 * INNER + pair * 128, 128)]
        parts = []
        for half in range(2):
            scores = dot(q * masks[half], k, NT) * 0.125
            free = jnp.where(allowed, jnp.exp(scores), 0.0)
            weights = free / jnp.sum(free, axis=-1, keepdims=True)
            s["weights"][2 * pair + half] = weights
            parts.append(dot(weights.astype(BF16), v))
        s["ctx"][:, lanes] = jnp.where(low, parts[0], parts[1]).astype(BF16)
    wait("wo")
    s["att"][...] = dot(s["ctx"][...], wo[...]).astype(BF16)


def diagonal(product, eye):
    return jnp.sum(jnp.where(eye, product, 0.0), axis=0, keepdims=True)


def by_sublane(rows):
    at = iota((8, T), 0) % 4
    block = jnp.broadcast_to(rows[3], (8, T))
    for k in range(3):
        block = jnp.where(at == k, jnp.broadcast_to(rows[k], (8, T)), block)
    return block


def adjoint_rows(g, s, out):
    def att_rows(block, _):
        rows = pl.ds(pl.multiple_of(block * ROWS, ROWS), ROWS)
        c = s["coef"][rows, :]
        total = c[:, 4:5] * g[0, rows, :].astype(F32)
        for i in range(1, LANES):
            total = total + c[:, 4 + i : 5 + i] * g[i, rows, :].astype(F32)
        out[rows, :] = total.astype(BF16)
        return 0

    lax.fori_loop(0, T // ROWS, att_rows, 0)


def attention_back(datt, wo, s, out):
    dctx = dot(datt[...], wo[...], NT).astype(BF16)
    low, masks = half_masks()
    ones = head_ones()

    def norm_back(dn, at):
        lanes = pl.ds(at * 128, 128)
        wide = s["proj"][:, lanes].astype(F32)
        scale = s["scale"][:, lanes]
        dn = dn.astype(BF16).astype(F32)
        moment = head_mean(dn * wide, ones)
        out[:, lanes] = (scale * (dn - wide * (scale * scale * moment))).astype(BF16)

    for pair in range(PAIRS):
        lanes = slice(pair * 128, pair * 128 + 128)
        q = s["qk"][:, pl.ds(pair * 128, 128)]
        key = s["qk"][:, pl.ds(INNER + pair * 128, 128)]
        v = s["proj"][:, pl.ds(2 * INNER + pair * 128, 128)]
        dc = dctx[:, lanes]
        dq, dk, dv = [], [], []
        for side in range(2):
            weights = s["weights"][2 * pair + side]
            dw = dot(dc * masks[side], v, NT).astype(BF16).astype(F32)
            dscore = weights * (dw - jnp.sum(dw * weights, axis=-1, keepdims=True)) * 0.125
            dq.append(dot(dscore.astype(BF16), key))
            dk.append(dot(dscore.T.astype(BF16), q))
            dv.append(dot(weights.T.astype(BF16), dc))
        out[:, pl.ds(2 * INNER + pair * 128, 128)] = jnp.where(low, dv[0], dv[1]).astype(BF16)
        norm_back(jnp.where(low, dq[0], dq[1]), pair)
        norm_back(jnp.where(low, dk[0], dk[1]), PAIRS + pair)


def stream_back(x, g, gain, w, s, o, t):
    eye = iota((T, T), 0) == iota((T, T), 1)
    t["dn"][...] = dot(o["dproj"][...], w[...], NT).astype(BF16)

    def joined_rows(block, total):
        rows = pl.ds(pl.multiple_of(block * ROWS, ROWS), ROWS)
        r = s["r"][rows, 0:1]
        joined = s["joined"][rows, :]
        dn = t["dn"][rows, :].astype(F32)
        total = total + jnp.sum(dn * (joined * r), axis=0, keepdims=True)
        scaled = dn * gain[...]
        moment = jnp.mean(scaled * joined, axis=-1, keepdims=True)
        t["dj"][rows, :] = r * scaled - joined * (r * r * r * moment)
        return total

    o["dgain"][...] = lax.fori_loop(0, T // ROWS, joined_rows, jnp.zeros((1, D), F32))

    dj = t["dj"][...].astype(BF16)
    pre = [diagonal(dot(dj, x[j], NT), eye) for j in range(LANES)]
    post = [diagonal(dot(g[i], s["att"][...], NT), eye) for i in range(LANES)]
    dmix = tuple(
        by_sublane([diagonal(dot(g[i], x[j], NT), eye) for j in range(LANES)])
        for i in range(LANES)
    )

    def one_round(step, current):
        index = SINK - 1 - step
        after = [s["sink"][index, 8 + i] for i in range(LANES)]
        pull = [a * b for a, b in zip(current, after)]
        pull = (pull[0] + pull[1]) + (pull[2] + pull[3])
        total = s["sink"][index, 12]
        current = [(a - pull) * total for a in current]
        between = [s["sink"][index, i] for i in range(LANES)]
        sums = [s["sink"][index, 4 + i] for i in range(LANES)]
        return tuple(
            (a - group_sum(a * b)) * c for a, b, c in zip(current, between, sums)
        )

    dmix = lax.fori_loop(0, SINK, one_round, dmix)
    lower = iota((8, T), 0) < 4
    mc = s["mc"][...]
    inv = mc[24:32]
    gates = jax.nn.sigmoid(mc[0:8])
    dgates = jnp.where(lower, by_sublane(pre), 2.0 * by_sublane(post))
    dmc = [
        dgates * gates * (1.0 - gates),
        jnp.where(lower, dmix[0], dmix[1]) * jnp.exp(mc[8:16]),
        jnp.where(lower, dmix[2], dmix[3]) * jnp.exp(mc[16:24]),
    ]
    dot_mc = dmc[0] * mc[0:8] + dmc[1] * mc[8:16] + dmc[2] * mc[16:24]
    dot_mc = jnp.sum(dot_mc, axis=0, keepdims=True)
    kappa = inv * inv * dot_mc * (1.0 / (LANES * D))
    scaled = jnp.concatenate([a * inv for a in dmc] + [jnp.zeros((8, T), F32)], axis=0)
    t["back"][...] = tokens_first(jnp.concatenate([scaled, scaled, kappa], axis=0))
    rows_first = scaled.astype(BF16)
    for j in range(LANES):
        o["dproj_map"][:, j * D : (j + 1) * D] = dot(rows_first, x[j])


def stream_out(x, g, bhl, s, t, put):
    lead = t["back"][:, 0:64].astype(BF16)
    for j in range(LANES):
        t["f"][j] = dot(lead, bhl[:, j * D : (j + 1) * D])

    def stream_rows(put, block, _):
        rows = pl.ds(pl.multiple_of(block * ROWS, ROWS), ROWS)
        c = s["coef"][rows, :]
        kap = t["back"][rows, 64:65]
        dj = t["dj"][rows, :]
        gs = [g[i, rows, :].astype(F32) for i in range(LANES)]
        for j in range(LANES):
            total = t["f"][j, rows, :] + c[:, j : j + 1] * dj - kap * x[j, rows, :].astype(F32)
            for i in range(LANES):
                at = 8 + LANES * i + j
                total = total + c[:, at : at + 1] * gs[i]
            put(block, j, total.astype(BF16))
        return 0

    for first, last, place in put:
        lax.fori_loop(first, last, functools.partial(stream_rows, place), 0)


SAVED = (
    ("mc", (32, T), F32),
    ("sink", (SINK, 13, 8, T), F32),
    ("coef", (T, 128), F32),
    ("joined", (T, D), F32),
    ("r", (T, 128), F32),
    ("proj", (T, 3 * INNER), BF16),
    ("scale", (T, 2 * INNER), F32),
    ("qk", (T, 2 * INNER), BF16),
    ("weights", (HEADS, T, T), F32),
    ("att", (T, D), BF16),
    ("bhl", (64, LANES * D), BF16),
)
LEFT_OUT = (("left", (T, LEFT), BF16),)
MAP = (("dproj_map", (32, LANES * D), F32), ("dgain", (1, D), F32))
CARRIED = (("dj", (T, D), F32), ("back", (T, 128), F32))
NORM = (("dn", (T, D), BF16),)
MAPPED = (("f", (LANES, T, D), F32),)
TEMPS = CARRIED + NORM + MAPPED
STREAMS = (("g", (LANES, T, D), BF16),)
VMEM = pl.BlockSpec(memory_space=pltpu.VMEM)
ANY = pl.BlockSpec(memory_space=pl.ANY)
SMEM = pl.BlockSpec(memory_space=pltpu.SMEM)


def struct(shape, dtype):
    return jax.ShapeDtypeStruct(shape, dtype)


def shapes(table):
    return [struct(shape, dtype) for _, shape, dtype in table]


def scratch(table):
    return [pltpu.VMEM(shape, dtype) for _, shape, dtype in table]


def names(table):
    return [name for name, _, _ in table]


def named(table, refs):
    return dict(zip(names(table), refs))


def call(body, outs, scratches, args, micros, name, specs=None):
    return pl.pallas_call(
        body,
        out_shape=outs,
        in_specs=specs or [VMEM] * len(args),
        out_specs=[VMEM] * len(outs),
        scratch_shapes=scratches,
        compiler_params=pltpu.CompilerParams(vmem_limit_bytes=56 * 1024 * 1024),
        cost_estimate=pl.CostEstimate(
            flops=micros * 1_000_000_000, bytes_accessed=micros * 2_000_000, transcendentals=0
        ),
        name=name,
    )(*args)


def brought(table, sources, rest, sem):
    buffers = named(table, rest)
    copies = {
        name: pltpu.make_async_copy(source, buffers[name], sem.at[k])
        for k, (name, source) in enumerate(zip(names(table), sources))
    }
    for copy in copies.values():
        copy.start()
    return buffers, lambda name: copies[name].wait()


def bring_adjoint(where, near, far, final, g, sem):
    parts = [g.at[:, pl.ds(0, FRONT), :], g.at[:, pl.ds(FRONT, T - FRONT), :]]
    last = [final.at[:, pl.ds(0, FRONT), :], final.at[:, pl.ds(FRONT, T - FRONT), :]]
    for case, sources in enumerate((near, far, last)):

        @pl.when(where[0] == case)
        def _(sources=sources):
            for k in range(2):
                pltpu.make_async_copy(sources[k], parts[k], sem.at[k]).start()

    def wait():
        for k in range(2):
            pltpu.make_async_copy(near[k], parts[k], sem.at[k]).wait()

    return wait


def factors(refs, right, left):
    if right is not None:
        refs["dproj"] = right.at[:, pl.ds(0, 3 * INNER)]
        refs["datt"] = right.at[:, pl.ds(3 * INNER, D)]
    if left is not None:
        refs["normed"] = left.at[:, pl.ds(0, D)]
        refs["ctx"] = left.at[:, pl.ds(D, INNER)]
    return refs


WEIGHTS = (("w", (D, 3 * INNER), BF16), ("wo", (INNER, D), BF16))
EARLY = (("x_rows", (T, LANES, D), BF16),)
LATE = EARLY + WEIGHTS + (("g_rows", (T, LANES, D), BF16),)
LANED = (("x", (LANES, T, D), BF16), ("g", (LANES, T, D), BF16))


def lanes_apart(source, out):
    def some_rows(block, _):
        rows = pl.ds(pl.multiple_of(block * ROWS, ROWS), ROWS)
        for j in range(LANES):
            out[j, rows, :] = source[rows, j, :]
        return 0

    lax.fori_loop(0, T // ROWS, some_rows, 0)


def whole_tick(x, g, seg, bt, gain, w, wo):
    outs = [
        ("dx_front", (LANES, FRONT, D), BF16),
        ("dx_back", (LANES, T - FRONT, D), BF16),
        ("right", (T, RIGHT), BF16),
        ("left", (T, LEFT), BF16),
        *MAP,
    ]

    def body(x, g, seg, bt, gain, w, wo, *rest):
        o = named(outs, rest)
        s = factors({}, None, o["left"])
        factors(o, o["right"], None)
        rest = rest[len(outs) :]
        s.update(named(SAVED, rest))
        t = named(TEMPS, rest[len(SAVED) :])
        rest = rest[len(SAVED) + len(TEMPS) :]
        buffers, wait = brought(LATE, (x.at[0], w, wo, g), rest, rest[-1])
        x_rows, w, wo, g_rows = (buffers[k] for k in names(LATE))
        laned = named(LANED, rest[len(LATE) :])
        wait("x_rows")
        lanes_apart(x_rows, laned["x"])
        x, g = laned["x"], laned["g"]
        stacked_map(bt, s["bhl"])
        forward(x, s["bhl"], gain, w, wo, seg.at[pl.ds(0, 1), :], s, wait)
        wait("g_rows")
        lanes_apart(g_rows, g)
        adjoint_rows(g, s, o["datt"])
        attention_back(o["datt"], wo, s, o["dproj"])

        def put_front(block, j, value):
            o["dx_front"][j, pl.ds(pl.multiple_of(block * ROWS, ROWS), ROWS), :] = value

        def put_back(block, j, value):
            at = pl.multiple_of(block * ROWS - FRONT, ROWS)
            o["dx_back"][j, pl.ds(at, ROWS), :] = value

        cut = FRONT // ROWS
        put = ((0, cut, put_front), (cut, T // ROWS, put_back))
        stream_back(x, g, gain, w, s, o, t)
        stream_out(x, g, s["bhl"], s, t, put)

    got = call(
        body,
        shapes(outs),
        scratch(SAVED)
        + scratch(TEMPS)
        + scratch(LATE)
        + scratch(LANED)
        + [pltpu.SemaphoreType.DMA((len(LATE),))],
        (x, g, seg, bt, gain, w, wo),
        20,
        "whole_tick",
        [ANY, ANY, VMEM, VMEM, VMEM, ANY, ANY],
    )
    return named(outs, got)


def forward_tick(x, seg, bt, gain, w, wo):
    table = SAVED + LEFT_OUT + LANED[:1]
    late = EARLY + WEIGHTS

    def body(x, seg, bt, gain, w, wo, *rest):
        s = named(table, rest)
        factors(s, None, s["left"])
        *rest, sem = rest[len(table) :]
        buffers, wait = brought(late, (x.at[1], w, wo), rest, sem)
        x_rows, w, wo = (buffers[k] for k in names(late))
        stacked_map(bt, s["bhl"])
        wait("x_rows")
        lanes_apart(x_rows, s["x"])
        forward(s["x"], s["bhl"], gain, w, wo, seg.at[pl.ds(1, 1), :], s, wait)

    got = call(
        body,
        shapes(table),
        scratch(late) + [pltpu.SemaphoreType.DMA((len(late),))],
        (x, seg, bt, gain, w, wo),
        FORWARD_COST,
        "forward_tick",
        [ANY, VMEM, VMEM, VMEM, ANY, ANY],
    )
    return named(table, got)


ATTENTION = [e for e in SAVED if e[0] in ("proj", "scale", "qk", "weights")]


def attention_tick(where, near, far, final, wo, saved, after):
    table = WEIGHTS[1:] + tuple(ATTENTION)

    def body(where, near0, near1, far0, far1, final, after, coef, *rest):
        sources, right, g = rest[: len(table)], rest[len(table)], rest[len(table) + 1]
        *buffers, g_sem, sem = rest[len(table) + 2 :]
        ready = bring_adjoint(where, (near0, near1), (far0, far1), final, g, g_sem)
        s, wait = brought(table, sources, buffers, sem)
        o = factors({}, right, None)
        ready()
        adjoint_rows(g, {"coef": coef}, o["datt"])
        for name in names(table):
            wait(name)
        attention_back(o["datt"], s["wo"], s, o["dproj"])

    args = (where, *near, *far, final, after, saved["coef"], wo, *[saved[k] for k in names(ATTENTION)])
    return call(
        body,
        [struct((T, RIGHT), BF16)],
        scratch(STREAMS)
        + scratch(table)
        + [pltpu.SemaphoreType.DMA((2,)), pltpu.SemaphoreType.DMA((len(table),))],
        args,
        5,
        "attention_tick",
        [SMEM] + [ANY] * 6 + [VMEM] + [ANY] * len(table),
    )[0]


REST = [e for e in SAVED if e[0] in ("mc", "sink", "joined", "r", "att")]


def stream_tick(x, adjoint, gain, w, right, saved, earlier, n, after):
    where, near, far, final = adjoint

    def body(where, near0, near1, far0, far1, final, after, x, gain, w, right, *rest):
        s = named(REST, rest)
        rest = rest[len(REST) :]
        first = named(MAP, rest)
        parts, *rest = rest[len(MAP) :]
        t = named(CARRIED, rest)
        rest = rest[len(CARRIED) :]
        o = named(MAP, rest)
        factors(o, right, None)
        rest = rest[len(MAP) :]
        t.update(named(NORM, rest))
        g, sem = rest[len(NORM) :]
        ready = bring_adjoint(where, (near0, near1), (far0, far1), final, g, sem)
        ready()
        stream_back(x, g, gain, w, s, o, t)
        width = LANES * D // n
        for d in range(n):
            cols = slice(d * width, d * width + width)
            proj = first["dproj_map"][:, cols] + o["dproj_map"][:, cols]
            lanes = slice(d * (D // n), (d + 1) * (D // n))
            total = first["dgain"][:, lanes] + o["dgain"][:, lanes]
            total = jnp.concatenate([total, jnp.zeros((1, width - D // n), F32)], axis=1)
            total = jnp.broadcast_to(total, (8, width))
            parts[d] = jnp.concatenate([proj[0:24], total], axis=0).astype(BF16)

    args = (where, *near, *far, final, after, x, gain, w, right)
    args += tuple(saved[k] for k in names(REST)) + tuple(earlier[k] for k in names(MAP))
    return call(
        body,
        [struct((n, 32, LANES * D // n), BF16)] + shapes(CARRIED),
        scratch(MAP) + scratch(NORM) + scratch(STREAMS) + [pltpu.SemaphoreType.DMA((2,))],
        args,
        6,
        "stream_tick",
        [SMEM] + [ANY] * 6 + [VMEM] * (4 + len(REST) + len(MAP)),
    )


def output_tick(x, adjoint, coef, bhl, dj, back, after):
    where, near, far, final = adjoint

    def body(where, near0, near1, far0, far1, final, after, x, coef, bhl, dj, back, dx, *rest):
        t = {"dj": dj, "back": back, "f": rest[0]}
        g, sem = rest[1:]
        ready = bring_adjoint(where, (near0, near1), (far0, far1), final, g, sem)
        ready()

        def put_rows(block, j, value):
            dx[j, pl.ds(pl.multiple_of(block * ROWS, ROWS), ROWS), :] = value

        stream_out(x, g, bhl, {"coef": coef}, t, ((0, T // ROWS, put_rows),))

    return call(
        body,
        [struct((LANES, T, D), BF16)],
        scratch(MAPPED) + scratch(STREAMS) + [pltpu.SemaphoreType.DMA((2,))],
        (where, *near, *far, final, after, x, coef, bhl, dj, back),
        5,
        "output_tick",
        [SMEM] + [ANY] * 6 + [VMEM] * 5,
    )[0]


STEPS = 4


def turned_factors(place, sides):
    rows, few = D // (2 * STEPS), INNER // (2 * STEPS)

    def body(place, *refs):
        refs, (left, small) = refs[:STEPS], refs[STEPS:]
        sides = [factors({}, None, side) for side in refs]
        even = place[STEPS] == 0
        for step in range(STEPS):
            chip = place[step]
            at = pl.multiple_of((2 * chip + place[STEPS]) * rows, rows)
            near = pl.multiple_of(chip * rows, rows)
            for k, side in enumerate(sides):
                tokens = slice(k * T, k * T + T)
                block = side["normed"][:, pl.ds(at, rows)].astype(F32).T
                left[step * rows : (step + 1) * rows, tokens] = block.astype(BF16)
                block = side["ctx"][:, pl.ds(near, rows)].astype(F32).T
                block = jnp.where(even, block[0:few], block[few:rows])
                small[step * few : (step + 1) * few, tokens] = block.astype(BF16)

    return call(
        body,
        [struct((STEPS * rows, STEPS * T), BF16), struct((STEPS * few, STEPS * T), BF16)],
        [],
        (place, *sides),
        FORWARD_COST,
        "turned_factors",
        [SMEM] + [VMEM] * STEPS,
    )


PACKED = 3 * INNER + D // 2


def terms(left, small, rights):
    rows, few = D // (2 * STEPS), INNER // (2 * STEPS)

    def body(left, small, *refs):
        rights, outs = refs[:STEPS], refs[STEPS:]

        def right(at):
            return jnp.concatenate([r[:, at : at + 256] for r in rights], axis=0)

        for at in range(0, 3 * INNER, 256):
            product = dot(left[...], right(at))
            for step in range(STEPS):
                part = product[step * rows : (step + 1) * rows]
                outs[step][:, at : at + 256] = part.astype(outs[step].dtype)
        for at in range(0, D, 256):
            product = dot(small[...], right(3 * INNER + at))
            top = few * (at // (D // 2))
            cols = 3 * INNER + at % (D // 2)
            for step in range(STEPS):
                part = product[step * few : (step + 1) * few]
                outs[step][top : top + few, cols : cols + 256] = part.astype(outs[step].dtype)

    own, *sends = call(
        body,
        [struct((rows, PACKED), F32)] + [struct((rows, PACKED), BF16)] * (STEPS - 1),
        [],
        (left, small, *rights),
        4,
        "terms",
    )
    return own, sends


def finish_terms(terms, after):
    few = INNER // (2 * STEPS)

    def body(*refs):
        *others, _, grad_qkv, grad_out = refs[1:]
        total = refs[0][...]
        for other in others:
            total = total + other[...].astype(F32)
        grad_qkv[...] = total[:, : 3 * INNER]
        grad_out[:, : D // 2] = total[:few, 3 * INNER :]
        grad_out[:, D // 2 :] = total[few:, 3 * INNER :]

    rows = terms[0].shape[0]
    outs = [struct((rows, 3 * INNER), F32), struct((few, D), F32)]
    specs = [VMEM] * len(terms) + [ANY]
    return call(body, outs, [], (*terms, after), 2, "finish_terms", specs)


def finish_map(parts, n):
    width = LANES * D // n

    def body(parts, grad_map, grad_gain):
        total = parts[0].astype(F32)
        for d in range(1, n):
            total = total + parts[d].astype(F32)
        grad_map[...] = total[0:24]
        grad_gain[...] = total[24:25, 0 : D // n]

    return call(
        body,
        [struct((24, width), F32), struct((1, D // n), F32)],
        [],
        (parts,),
        1,
        "finish_map",
    )


def shards(
    saved_entering_lanes,
    opening_adjoint,
    final_later_adjoint,
    document_labels,
    blend_linear_map,
    rescale_amplitude,
    attend_entry_maps,
    attend_exit_map,
):
    n = lax.axis_size("dp")
    layers = lax.axis_size("section")
    section = lax.axis_index("section")
    replica = lax.axis_index("dp")
    chip, core = replica // 2, replica % 2
    lanes_first = lambda a: jnp.transpose(a, (1, 0, 2))
    x = saved_entering_lanes[0]
    opening = opening_adjoint[0]
    final = lanes_first(final_later_adjoint[0])
    bt = blend_linear_map[0].T
    gain = rescale_amplitude
    w = attend_entry_maps[0]
    wo = attend_exit_map[0]

    def swap_cores(value):
        return lax.ppermute(value, "dp", [(i, i ^ 1) for i in range(n)])

    def along(value, *chips):
        route = [(2 * a + c, 2 * b + c) for a, b in chips for c in range(2)]
        return lax.ppermute(value, "dp", route)

    first = whole_tick(x, opening, document_labels[0], bt, gain, w, wo)

    near = [(s, s - 1) for s in range(1, layers) if s % RUN]
    cross = range(RUN, layers, RUN)
    hop = lax.ppermute(first["dx_back"], "section", near + [(s, s + RUN - 1) for s in cross])
    front_far = lax.ppermute(first["dx_front"], "section", [(s, s - 1) for s in cross])
    others_left, others_right = swap_cores(first["left"]), swap_cores(first["right"])
    saved = forward_tick(x, document_labels[0], bt, gain, w, wo)
    coming, later, _ = lax.optimization_barrier((hop, first["dx_front"], saved["coef"]))
    far = lax.ppermute(coming, "section", [(s + RUN - 1, s - 1) for s in cross])
    front_near = lax.ppermute(later, "section", near)
    place = jnp.stack([chip ^ step for step in range(STEPS)] + [core])
    left, small = turned_factors(
        place, (first["left"], saved["left"], others_left, swap_cores(saved["left"]))
    )
    where = jnp.where(section == layers - 1, 2, jnp.where(section % RUN == RUN - 1, 1, 0))
    adjoint = (where[None], (front_near, hop), (front_far, far), final)
    right = attention_tick(*adjoint, wo, saved, left)
    own, sends = terms(left, small, [first["right"], right, others_right, swap_cores(right)])
    by_way = along(sends[2], (0, 1), (3, 2))
    middle = along(sends[2], (1, 2), (2, 1))
    beside = along(sends[0], (0, 1), (1, 0), (2, 3), (3, 2))
    outer = along(sends[1], (0, 2), (3, 1))
    parts, dj, back = stream_tick(saved["x"], adjoint, gain, w, right, saved, first, n, own)
    by_way, parts = lax.optimization_barrier((by_way, parts))
    both = (sends[1].astype(F32) + by_way.astype(F32)).astype(BF16)
    grads = [own, middle, beside, outer, along(both, (1, 3), (2, 0))]
    dx1 = output_tick(saved["x"], adjoint, saved["coef"], saved["bhl"], dj, back, both)
    parts = lax.all_to_all(parts, "dp", 0, 0)
    grad_map, grad_gain = finish_map(parts, n)
    grad_qkv, grad_out = finish_terms(grads, grad_map)
    dx0 = jnp.concatenate([first["dx_front"], first["dx_back"]], axis=1)
    sent = jnp.stack([jnp.transpose(dx0, (1, 0, 2)), jnp.transpose(dx1, (1, 0, 2))])[None]
    return (sent, grad_qkv[None], grad_out[None], grad_map.T[None], grad_gain)


def solution(mesh):
    return jax.shard_map(
        shards,
        mesh=mesh,
        in_specs=(
            P("section", None, "dp", None, None),
            P("section", "dp", None, None),
            P(None, "dp", None, None),
            P("section", None, "dp"),
            P("section", None, None),
            P("section", None),
            P("section", None, None),
            P("section", None, None),
        ),
        out_specs=(
            P("section", None, "dp", None, None),
            P("section", "dp", None),
            P("section", "dp", None),
            P("section", "dp", None),
            P("section", "dp"),
        ),
        check_vma=False,
    )
```

```python
import functools

import jax
import jax.numpy as jnp
from jax import lax
from jax.experimental import pallas as pl
from jax.experimental.pallas import tpu as pltpu
from jax.sharding import PartitionSpec as P

F32 = jnp.float32
BF16 = jnp.bfloat16
LANES = 4
D = 1024
T = 128
HEADS = 8
PAIRS = HEADS // 2
INNER = 512
SINK = 20
EPS = 1e-6
ROWS = 16
RUN = 4
FORWARD_COST = 1
RIGHT = 3 * INNER + D
LEFT = D + INNER
FRONT = 80
NN = (((1,), (0,)), ((), ()))
NT = (((1,), (1,)), ((), ()))
TN = (((0,), (0,)), ((), ()))


def dot(a, b, dims=NN):
    return lax.dot_general(a, b, dims, preferred_element_type=F32)


def split(value):
    high = value.astype(BF16)
    return high, (value - high.astype(F32)).astype(BF16)


def iota(shape, axis):
    return lax.broadcasted_iota(jnp.int32, shape, axis)


def group_sum(block):
    block = block + pltpu.roll(block, 1, 0)
    return block + pltpu.roll(block, 2, 0)


def doubled(block):
    lower = iota(block.shape, 0) < 4
    turned = pltpu.roll(block, 4, 0)
    return jnp.where(lower, block, turned), jnp.where(lower, turned, block)


def tokens_first(rows):
    short = 128 - rows.shape[0]
    if short:
        rows = jnp.concatenate([rows, jnp.zeros((short, T), F32)], axis=0)
    return rows.T


def head_ones():
    return (iota((128, 128), 0) // 64 == iota((128, 128), 1) // 64).astype(BF16)


def head_mean(value, ones):
    high, low = split(value)
    return (dot(high, ones) + dot(low, ones)) * (1.0 / 64.0)


def half_masks():
    low = iota((1, 128), 1) < 64
    return low, [low.astype(F32).astype(BF16), (~low).astype(F32).astype(BF16)]


def stacked_map(bt_ref, bhl):
    high, low = split(jnp.concatenate([bt_ref[...], jnp.zeros((8, LANES * D), F32)], axis=0))
    bhl[0:32, :] = high
    bhl[32:64, :] = low


def forward(x, bhl, gain, w, wo, seg, s, wait):
    eye = iota((T, T), 0) == iota((T, T), 1)
    raw = jnp.zeros((64, T), F32)
    square = jnp.zeros((T, T), F32)
    for j in range(LANES):
        raw = raw + dot(bhl[:, j * D : (j + 1) * D], x[j], NT)
        square = square + dot(x[j], x[j], NT)
    mean = jnp.sum(jnp.where(eye, square, 0.0), axis=0, keepdims=True) * (1.0 / (LANES * D))
    inv = lax.rsqrt(mean + EPS)
    mc = (raw[0:24] + raw[32:56]) * inv
    s["mc"][...] = jnp.concatenate([mc, jnp.broadcast_to(inv, (8, T))], axis=0)
    lower = iota((8, T), 0) < 4
    gates = jax.nn.sigmoid(mc[0:8])
    gates = jnp.where(lower, gates, 2.0 * gates)
    first = doubled(jnp.exp(mc[8:16]))
    second = doubled(jnp.exp(mc[16:24]))

    def one_round(index, current):
        sums = [1.0 / group_sum(a) for a in current]
        current = [a * b for a, b in zip(current, sums)]
        for i in range(LANES):
            s["sink"][index, i] = current[i]
            s["sink"][index, 4 + i] = sums[i]
        total = 1.0 / ((current[0] + current[1]) + (current[2] + current[3]))
        current = [a * total for a in current]
        for i in range(LANES):
            s["sink"][index, 8 + i] = current[i]
        s["sink"][index, 12] = total
        return tuple(current)

    settled = lax.fori_loop(0, SINK, one_round, first + second)
    s["coef"][...] = tokens_first(
        jnp.concatenate(
            [
                gates,
                jnp.where(lower, settled[0], settled[1]),
                jnp.where(lower, settled[2], settled[3]),
            ],
            axis=0,
        )
    )

    def join_rows(block, _):
        rows = pl.ds(pl.multiple_of(block * ROWS, ROWS), ROWS)
        c = s["coef"][rows, :]
        joined = c[:, 0:1] * x[0, rows, :].astype(F32)
        for i in range(1, LANES):
            joined = joined + c[:, i : i + 1] * x[i, rows, :].astype(F32)
        r = lax.rsqrt(jnp.mean(joined * joined, axis=-1, keepdims=True) + EPS)
        s["joined"][rows, :] = joined
        s["r"][rows, :] = jnp.broadcast_to(r, (ROWS, 128))
        s["normed"][rows, :] = (joined * r * gain[...]).astype(BF16)
        return 0

    lax.fori_loop(0, T // ROWS, join_rows, 0)
    wait("w")
    projected = dot(s["normed"][...], w[...]).astype(BF16)
    s["proj"][...] = projected
    ones = head_ones()
    for at in range(2 * PAIRS):
        lanes = slice(at * 128, at * 128 + 128)
        wide = projected[:, lanes].astype(F32)
        scale = lax.rsqrt(head_mean(wide * wide, ones) + EPS)
        s["scale"][:, lanes] = scale
        s["qk"][:, lanes] = (wide * scale).astype(BF16)
    ids = jnp.broadcast_to(seg[...].astype(F32), (T, T))
    allowed = (ids == ids.T) & (iota((T, T), 1) <= iota((T, T), 0))
    low, masks = half_masks()
    for pair in range(PAIRS):
        lanes = slice(pair * 128, pair * 128 + 128)
        q = s["qk"][:, lanes]
        k = s["qk"][:, pl.ds(INNER + pair * 128, 128)]
        v = s["proj"][:, pl.ds(2 * INNER + pair * 128, 128)]
        parts = []
        for half in range(2):
            scores = dot(q * masks[half], k, NT) * 0.125
            free = jnp.where(allowed, jnp.exp(scores), 0.0)
            weights = free / jnp.sum(free, axis=-1, keepdims=True)
            s["weights"][2 * pair + half] = weights
            parts.append(dot(weights.astype(BF16), v))
        s["ctx"][:, lanes] = jnp.where(low, parts[0], parts[1]).astype(BF16)
    wait("wo")
    s["att"][...] = dot(s["ctx"][...], wo[...]).astype(BF16)


def diagonal(product, eye):
    return jnp.sum(jnp.where(eye, product, 0.0), axis=0, keepdims=True)


def by_sublane(rows):
    at = iota((8, T), 0) % 4
    block = jnp.broadcast_to(rows[3], (8, T))
    for k in range(3):
        block = jnp.where(at == k, jnp.broadcast_to(rows[k], (8, T)), block)
    return block


def adjoint_rows(g, s, out):
    def att_rows(block, _):
        rows = pl.ds(pl.multiple_of(block * ROWS, ROWS), ROWS)
        c = s["coef"][rows, :]
        total = c[:, 4:5] * g[0, rows, :].astype(F32)
        for i in range(1, LANES):
            total = total + c[:, 4 + i : 5 + i] * g[i, rows, :].astype(F32)
        out[rows, :] = total.astype(BF16)
        return 0

    lax.fori_loop(0, T // ROWS, att_rows, 0)


def attention_back(datt, wo, s, out):
    dctx = dot(datt[...], wo[...], NT).astype(BF16)
    low, masks = half_masks()
    ones = head_ones()

    def norm_back(dn, at):
        lanes = pl.ds(at * 128, 128)
        wide = s["proj"][:, lanes].astype(F32)
        scale = s["scale"][:, lanes]
        dn = dn.astype(BF16).astype(F32)
        moment = head_mean(dn * wide, ones)
        out[:, lanes] = (scale * (dn - wide * (scale * scale * moment))).astype(BF16)

    for pair in range(PAIRS):
        lanes = slice(pair * 128, pair * 128 + 128)
        q = s["qk"][:, pl.ds(pair * 128, 128)]
        key = s["qk"][:, pl.ds(INNER + pair * 128, 128)]
        v = s["proj"][:, pl.ds(2 * INNER + pair * 128, 128)]
        dc = dctx[:, lanes]
        dq, dk, dv = [], [], []
        for side in range(2):
            weights = s["weights"][2 * pair + side]
            dw = dot(dc * masks[side], v, NT).astype(BF16).astype(F32)
            dscore = weights * (dw - jnp.sum(dw * weights, axis=-1, keepdims=True)) * 0.125
            dq.append(dot(dscore.astype(BF16), key))
            dk.append(dot(dscore.T.astype(BF16), q))
            dv.append(dot(weights.T.astype(BF16), dc))
        out[:, pl.ds(2 * INNER + pair * 128, 128)] = jnp.where(low, dv[0], dv[1]).astype(BF16)
        norm_back(jnp.where(low, dq[0], dq[1]), pair)
        norm_back(jnp.where(low, dk[0], dk[1]), PAIRS + pair)


def stream_back(x, g, gain, w, s, o, t):
    eye = iota((T, T), 0) == iota((T, T), 1)
    t["dn"][...] = dot(o["dproj"][...], w[...], NT).astype(BF16)

    def joined_rows(block, total):
        rows = pl.ds(pl.multiple_of(block * ROWS, ROWS), ROWS)
        r = s["r"][rows, 0:1]
        joined = s["joined"][rows, :]
        dn = t["dn"][rows, :].astype(F32)
        total = total + jnp.sum(dn * (joined * r), axis=0, keepdims=True)
        scaled = dn * gain[...]
        moment = jnp.mean(scaled * joined, axis=-1, keepdims=True)
        t["dj"][rows, :] = r * scaled - joined * (r * r * r * moment)
        return total

    o["dgain"][...] = lax.fori_loop(0, T // ROWS, joined_rows, jnp.zeros((1, D), F32))

    dj = t["dj"][...].astype(BF16)
    pre = [diagonal(dot(dj, x[j], NT), eye) for j in range(LANES)]
    post = [diagonal(dot(g[i], s["att"][...], NT), eye) for i in range(LANES)]
    dmix = tuple(
        by_sublane([diagonal(dot(g[i], x[j], NT), eye) for j in range(LANES)])
        for i in range(LANES)
    )

    def one_round(step, current):
        index = SINK - 1 - step
        after = [s["sink"][index, 8 + i] for i in range(LANES)]
        pull = [a * b for a, b in zip(current, after)]
        pull = (pull[0] + pull[1]) + (pull[2] + pull[3])
        total = s["sink"][index, 12]
        current = [(a - pull) * total for a in current]
        between = [s["sink"][index, i] for i in range(LANES)]
        sums = [s["sink"][index, 4 + i] for i in range(LANES)]
        return tuple(
            (a - group_sum(a * b)) * c for a, b, c in zip(current, between, sums)
        )

    dmix = lax.fori_loop(0, SINK, one_round, dmix)
    lower = iota((8, T), 0) < 4
    mc = s["mc"][...]
    inv = mc[24:32]
    gates = jax.nn.sigmoid(mc[0:8])
    dgates = jnp.where(lower, by_sublane(pre), 2.0 * by_sublane(post))
    dmc = [
        dgates * gates * (1.0 - gates),
        jnp.where(lower, dmix[0], dmix[1]) * jnp.exp(mc[8:16]),
        jnp.where(lower, dmix[2], dmix[3]) * jnp.exp(mc[16:24]),
    ]
    dot_mc = dmc[0] * mc[0:8] + dmc[1] * mc[8:16] + dmc[2] * mc[16:24]
    dot_mc = jnp.sum(dot_mc, axis=0, keepdims=True)
    kappa = inv * inv * dot_mc * (1.0 / (LANES * D))
    scaled = jnp.concatenate([a * inv for a in dmc] + [jnp.zeros((8, T), F32)], axis=0)
    t["back"][...] = tokens_first(jnp.concatenate([scaled, scaled, kappa], axis=0))
    rows_first = scaled.astype(BF16)
    for j in range(LANES):
        o["dproj_map"][:, j * D : (j + 1) * D] = dot(rows_first, x[j])


def stream_out(x, g, bhl, s, t, put):
    lead = t["back"][:, 0:64].astype(BF16)
    for j in range(LANES):
        t["f"][j] = dot(lead, bhl[:, j * D : (j + 1) * D])

    def stream_rows(put, block, _):
        rows = pl.ds(pl.multiple_of(block * ROWS, ROWS), ROWS)
        c = s["coef"][rows, :]
        kap = t["back"][rows, 64:65]
        dj = t["dj"][rows, :]
        gs = [g[i, rows, :].astype(F32) for i in range(LANES)]
        for j in range(LANES):
            total = t["f"][j, rows, :] + c[:, j : j + 1] * dj - kap * x[j, rows, :].astype(F32)
            for i in range(LANES):
                at = 8 + LANES * i + j
                total = total + c[:, at : at + 1] * gs[i]
            put(block, j, total.astype(BF16))
        return 0

    for first, last, place in put:
        lax.fori_loop(first, last, functools.partial(stream_rows, place), 0)


SAVED = (
    ("mc", (32, T), F32),
    ("sink", (SINK, 13, 8, T), F32),
    ("coef", (T, 128), F32),
    ("joined", (T, D), F32),
    ("r", (T, 128), F32),
    ("proj", (T, 3 * INNER), BF16),
    ("scale", (T, 2 * INNER), F32),
    ("qk", (T, 2 * INNER), BF16),
    ("weights", (HEADS, T, T), F32),
    ("att", (T, D), BF16),
    ("bhl", (64, LANES * D), BF16),
)
LEFT_OUT = (("left", (T, LEFT), BF16),)
MAP = (("dproj_map", (32, LANES * D), F32), ("dgain", (1, D), F32))
CARRIED = (("dj", (T, D), F32), ("back", (T, 128), F32))
NORM = (("dn", (T, D), BF16),)
MAPPED = (("f", (LANES, T, D), F32),)
TEMPS = CARRIED + NORM + MAPPED
STREAMS = (("g", (LANES, T, D), BF16),)
VMEM = pl.BlockSpec(memory_space=pltpu.VMEM)
ANY = pl.BlockSpec(memory_space=pl.ANY)
SMEM = pl.BlockSpec(memory_space=pltpu.SMEM)


def struct(shape, dtype):
    return jax.ShapeDtypeStruct(shape, dtype)


def shapes(table):
    return [struct(shape, dtype) for _, shape, dtype in table]


def scratch(table):
    return [pltpu.VMEM(shape, dtype) for _, shape, dtype in table]


def names(table):
    return [name for name, _, _ in table]


def named(table, refs):
    return dict(zip(names(table), refs))


def call(body, outs, scratches, args, micros, name, specs=None):
    return pl.pallas_call(
        body,
        out_shape=outs,
        in_specs=specs or [VMEM] * len(args),
        out_specs=[VMEM] * len(outs),
        scratch_shapes=scratches,
        compiler_params=pltpu.CompilerParams(vmem_limit_bytes=56 * 1024 * 1024),
        cost_estimate=pl.CostEstimate(
            flops=micros * 1_000_000_000, bytes_accessed=micros * 2_000_000, transcendentals=0
        ),
        name=name,
    )(*args)


def brought(table, sources, rest, sem):
    buffers = named(table, rest)
    copies = {
        name: pltpu.make_async_copy(source, buffers[name], sem.at[k])
        for k, (name, source) in enumerate(zip(names(table), sources))
    }
    for copy in copies.values():
        copy.start()
    return buffers, lambda name: copies[name].wait()


def bring_adjoint(where, near, far, final, g, sem):
    parts = [g.at[:, pl.ds(0, FRONT), :], g.at[:, pl.ds(FRONT, T - FRONT), :]]
    last = [final.at[:, pl.ds(0, FRONT), :], final.at[:, pl.ds(FRONT, T - FRONT), :]]
    for case, sources in enumerate((near, far, last)):

        @pl.when(where[0] == case)
        def _(sources=sources):
            for k in range(2):
                pltpu.make_async_copy(sources[k], parts[k], sem.at[k]).start()

    def wait():
        for k in range(2):
            pltpu.make_async_copy(near[k], parts[k], sem.at[k]).wait()

    return wait


def factors(refs, right, left):
    if right is not None:
        refs["dproj"] = right.at[:, pl.ds(0, 3 * INNER)]
        refs["datt"] = right.at[:, pl.ds(3 * INNER, D)]
    if left is not None:
        refs["normed"] = left.at[:, pl.ds(0, D)]
        refs["ctx"] = left.at[:, pl.ds(D, INNER)]
    return refs


WEIGHTS = (("w", (D, 3 * INNER), BF16), ("wo", (INNER, D), BF16))
EARLY = (("x_rows", (T, LANES, D), BF16),)
LATE = EARLY + WEIGHTS + (("g_rows", (T, LANES, D), BF16),)
LANED = (("x", (LANES, T, D), BF16), ("g", (LANES, T, D), BF16))


def lanes_apart(source, out):
    def some_rows(block, _):
        rows = pl.ds(pl.multiple_of(block * ROWS, ROWS), ROWS)
        for j in range(LANES):
            out[j, rows, :] = source[rows, j, :]
        return 0

    lax.fori_loop(0, T // ROWS, some_rows, 0)


def whole_tick(x, g, seg, bt, gain, w, wo):
    outs = [
        ("dx_front", (LANES, FRONT, D), BF16),
        ("dx_back", (LANES, T - FRONT, D), BF16),
        ("right", (T, RIGHT), BF16),
        ("left", (T, LEFT), BF16),
        *MAP,
    ]

    def body(x, g, seg, bt, gain, w, wo, *rest):
        o = named(outs, rest)
        s = factors({}, None, o["left"])
        factors(o, o["right"], None)
        rest = rest[len(outs) :]
        s.update(named(SAVED, rest))
        t = named(TEMPS, rest[len(SAVED) :])
        rest = rest[len(SAVED) + len(TEMPS) :]
        buffers, wait = brought(LATE, (x.at[0], w, wo, g), rest, rest[-1])
        x_rows, w, wo, g_rows = (buffers[k] for k in names(LATE))
        laned = named(LANED, rest[len(LATE) :])
        wait("x_rows")
        lanes_apart(x_rows, laned["x"])
        x, g = laned["x"], laned["g"]
        stacked_map(bt, s["bhl"])
        forward(x, s["bhl"], gain, w, wo, seg.at[pl.ds(0, 1), :], s, wait)
        wait("g_rows")
        lanes_apart(g_rows, g)
        adjoint_rows(g, s, o["datt"])
        attention_back(o["datt"], wo, s, o["dproj"])

        def put_front(block, j, value):
            o["dx_front"][j, pl.ds(pl.multiple_of(block * ROWS, ROWS), ROWS), :] = value

        def put_back(block, j, value):
            at = pl.multiple_of(block * ROWS - FRONT, ROWS)
            o["dx_back"][j, pl.ds(at, ROWS), :] = value

        cut = FRONT // ROWS
        put = ((0, cut, put_front), (cut, T // ROWS, put_back))
        stream_back(x, g, gain, w, s, o, t)
        stream_out(x, g, s["bhl"], s, t, put)

    got = call(
        body,
        shapes(outs),
        scratch(SAVED)
        + scratch(TEMPS)
        + scratch(LATE)
        + scratch(LANED)
        + [pltpu.SemaphoreType.DMA((len(LATE),))],
        (x, g, seg, bt, gain, w, wo),
        20,
        "whole_tick",
        [ANY, ANY, VMEM, VMEM, VMEM, ANY, ANY],
    )
    return named(outs, got)


def forward_tick(x, seg, bt, gain, w, wo):
    table = SAVED + LEFT_OUT + LANED[:1]
    late = EARLY + WEIGHTS

    def body(x, seg, bt, gain, w, wo, *rest):
        s = named(table, rest)
        factors(s, None, s["left"])
        *rest, sem = rest[len(table) :]
        buffers, wait = brought(late, (x.at[1], w, wo), rest, sem)
        x_rows, w, wo = (buffers[k] for k in names(late))
        stacked_map(bt, s["bhl"])
        wait("x_rows")
        lanes_apart(x_rows, s["x"])
        forward(s["x"], s["bhl"], gain, w, wo, seg.at[pl.ds(1, 1), :], s, wait)

    got = call(
        body,
        shapes(table),
        scratch(late) + [pltpu.SemaphoreType.DMA((len(late),))],
        (x, seg, bt, gain, w, wo),
        FORWARD_COST,
        "forward_tick",
        [ANY, VMEM, VMEM, VMEM, ANY, ANY],
    )
    return named(table, got)


ATTENTION = [e for e in SAVED if e[0] in ("proj", "scale", "qk", "weights")]


def attention_tick(where, near, far, final, wo, saved, after):
    table = WEIGHTS[1:] + tuple(ATTENTION)

    def body(where, near0, near1, far0, far1, final, after, coef, *rest):
        sources, right, g = rest[: len(table)], rest[len(table)], rest[len(table) + 1]
        *buffers, g_sem, sem = rest[len(table) + 2 :]
        ready = bring_adjoint(where, (near0, near1), (far0, far1), final, g, g_sem)
        s, wait = brought(table, sources, buffers, sem)
        o = factors({}, right, None)
        ready()
        adjoint_rows(g, {"coef": coef}, o["datt"])
        for name in names(table):
            wait(name)
        attention_back(o["datt"], s["wo"], s, o["dproj"])

    args = (where, *near, *far, final, after, saved["coef"], wo, *[saved[k] for k in names(ATTENTION)])
    return call(
        body,
        [struct((T, RIGHT), BF16)],
        scratch(STREAMS)
        + scratch(table)
        + [pltpu.SemaphoreType.DMA((2,)), pltpu.SemaphoreType.DMA((len(table),))],
        args,
        5,
        "attention_tick",
        [SMEM] + [ANY] * 6 + [VMEM] + [ANY] * len(table),
    )[0]


REST = [e for e in SAVED if e[0] in ("mc", "sink", "joined", "r", "att")]


def stream_tick(x, adjoint, gain, w, right, saved, earlier, n, after):
    where, near, far, final = adjoint

    def body(where, near0, near1, far0, far1, final, after, x, gain, w, right, *rest):
        s = named(REST, rest)
        rest = rest[len(REST) :]
        first = named(MAP, rest)
        parts, *rest = rest[len(MAP) :]
        t = named(CARRIED, rest)
        rest = rest[len(CARRIED) :]
        o = named(MAP, rest)
        factors(o, right, None)
        rest = rest[len(MAP) :]
        t.update(named(NORM, rest))
        g, sem = rest[len(NORM) :]
        ready = bring_adjoint(where, (near0, near1), (far0, far1), final, g, sem)
        ready()
        stream_back(x, g, gain, w, s, o, t)
        width = LANES * D // n
        for d in range(n):
            cols = slice(d * width, d * width + width)
            proj = first["dproj_map"][:, cols] + o["dproj_map"][:, cols]
            lanes = slice(d * (D // n), (d + 1) * (D // n))
            total = first["dgain"][:, lanes] + o["dgain"][:, lanes]
            total = jnp.concatenate([total, jnp.zeros((1, width - D // n), F32)], axis=1)
            total = jnp.broadcast_to(total, (8, width))
            parts[d] = jnp.concatenate([proj[0:24], total], axis=0).astype(BF16)

    args = (where, *near, *far, final, after, x, gain, w, right)
    args += tuple(saved[k] for k in names(REST)) + tuple(earlier[k] for k in names(MAP))
    return call(
        body,
        [struct((n, 32, LANES * D // n), BF16)] + shapes(CARRIED),
        scratch(MAP) + scratch(NORM) + scratch(STREAMS) + [pltpu.SemaphoreType.DMA((2,))],
        args,
        6,
        "stream_tick",
        [SMEM] + [ANY] * 6 + [VMEM] * (4 + len(REST) + len(MAP)),
    )


def output_tick(x, adjoint, coef, bhl, dj, back, after):
    where, near, far, final = adjoint

    def body(where, near0, near1, far0, far1, final, after, x, coef, bhl, dj, back, dx, *rest):
        t = {"dj": dj, "back": back, "f": rest[0]}
        g, sem = rest[1:]
        ready = bring_adjoint(where, (near0, near1), (far0, far1), final, g, sem)
        ready()

        def put_rows(block, j, value):
            dx[j, pl.ds(pl.multiple_of(block * ROWS, ROWS), ROWS), :] = value

        stream_out(x, g, bhl, {"coef": coef}, t, ((0, T // ROWS, put_rows),))

    return call(
        body,
        [struct((LANES, T, D), BF16)],
        scratch(MAPPED) + scratch(STREAMS) + [pltpu.SemaphoreType.DMA((2,))],
        (where, *near, *far, final, after, x, coef, bhl, dj, back),
        5,
        "output_tick",
        [SMEM] + [ANY] * 6 + [VMEM] * 5,
    )[0]


STEPS = 4


def turned_factors(place, sides):
    rows, few = D // (2 * STEPS), INNER // (2 * STEPS)

    def body(place, *refs):
        refs, (left, small) = refs[:STEPS], refs[STEPS:]
        sides = [factors({}, None, side) for side in refs]
        even = place[STEPS] == 0
        for step in range(STEPS):
            chip = place[step]
            at = pl.multiple_of((2 * chip + place[STEPS]) * rows, rows)
            near = pl.multiple_of(chip * rows, rows)
            for k, side in enumerate(sides):
                tokens = slice(k * T, k * T + T)
                block = side["normed"][:, pl.ds(at, rows)].astype(F32).T
                left[step * rows : (step + 1) * rows, tokens] = block.astype(BF16)
                block = side["ctx"][:, pl.ds(near, rows)].astype(F32).T
                block = jnp.where(even, block[0:few], block[few:rows])
                small[step * few : (step + 1) * few, tokens] = block.astype(BF16)

    return call(
        body,
        [struct((STEPS * rows, STEPS * T), BF16), struct((STEPS * few, STEPS * T), BF16)],
        [],
        (place, *sides),
        FORWARD_COST,
        "turned_factors",
        [SMEM] + [VMEM] * STEPS,
    )


PACKED = 3 * INNER + D // 2


def terms(left, small, rights):
    rows, few = D // (2 * STEPS), INNER // (2 * STEPS)

    def body(left, small, *refs):
        rights, outs = refs[:STEPS], refs[STEPS:]

        def right(at):
            return jnp.concatenate([r[:, at : at + 256] for r in rights], axis=0)

        for at in range(0, 3 * INNER, 256):
            product = dot(left[...], right(at))
            for step in range(STEPS):
                part = product[step * rows : (step + 1) * rows]
                outs[step][:, at : at + 256] = part.astype(outs[step].dtype)
        for at in range(0, D, 256):
            product = dot(small[...], right(3 * INNER + at))
            top = few * (at // (D // 2))
            cols = 3 * INNER + at % (D // 2)
            for step in range(STEPS):
                part = product[step * few : (step + 1) * few]
                outs[step][top : top + few, cols : cols + 256] = part.astype(outs[step].dtype)

    own, *sends = call(
        body,
        [struct((rows, PACKED), F32)] + [struct((rows, PACKED), BF16)] * (STEPS - 1),
        [],
        (left, small, *rights),
        4,
        "terms",
    )
    return own, sends


def finish_terms(terms, after):
    few = INNER // (2 * STEPS)

    def body(*refs):
        *others, _, grad_qkv, grad_out = refs[1:]
        total = refs[0][...]
        for other in others:
            total = total + other[...].astype(F32)
        grad_qkv[...] = total[:, : 3 * INNER]
        grad_out[:, : D // 2] = total[:few, 3 * INNER :]
        grad_out[:, D // 2 :] = total[few:, 3 * INNER :]

    rows = terms[0].shape[0]
    outs = [struct((rows, 3 * INNER), F32), struct((few, D), F32)]
    specs = [VMEM] * len(terms) + [ANY]
    return call(body, outs, [], (*terms, after), 2, "finish_terms", specs)


def finish_map(parts, n):
    width = LANES * D // n

    def body(parts, grad_map, grad_gain):
        total = parts[0].astype(F32)
        for d in range(1, n):
            total = total + parts[d].astype(F32)
        grad_map[...] = total[0:24]
        grad_gain[...] = total[24:25, 0 : D // n]

    return call(
        body,
        [struct((24, width), F32), struct((1, D // n), F32)],
        [],
        (parts,),
        1,
        "finish_map",
    )


def shards(
    saved_entering_lanes,
    opening_adjoint,
    final_later_adjoint,
    document_labels,
    blend_linear_map,
    rescale_amplitude,
    attend_entry_maps,
    attend_exit_map,
):
    n = lax.axis_size("dp")
    layers = lax.axis_size("section")
    section = lax.axis_index("section")
    replica = lax.axis_index("dp")
    chip, core = replica // 2, replica % 2
    lanes_first = lambda a: jnp.transpose(a, (1, 0, 2))
    x = saved_entering_lanes[0]
    opening = opening_adjoint[0]
    final = lanes_first(final_later_adjoint[0])
    bt = blend_linear_map[0].T
    gain = rescale_amplitude
    w = attend_entry_maps[0]
    wo = attend_exit_map[0]

    def swap_cores(value):
        return lax.ppermute(value, "dp", [(i, i ^ 1) for i in range(n)])

    def along(value, *chips):
        route = [(2 * a + c, 2 * b + c) for a, b in chips for c in range(2)]
        return lax.ppermute(value, "dp", route)

    first = whole_tick(x, opening, document_labels[0], bt, gain, w, wo)

    near = [(s, s - 1) for s in range(1, layers) if s % RUN]
    cross = range(RUN, layers, RUN)
    hop = lax.ppermute(first["dx_back"], "section", near + [(s, s + RUN - 1) for s in cross])
    front_far = lax.ppermute(first["dx_front"], "section", [(s, s - 1) for s in cross])
    others_left, others_right = swap_cores(first["left"]), swap_cores(first["right"])
    saved = forward_tick(x, document_labels[0], bt, gain, w, wo)
    coming, later, _ = lax.optimization_barrier((hop, first["dx_front"], saved["coef"]))
    far = lax.ppermute(coming, "section", [(s + RUN - 1, s - 1) for s in cross])
    front_near = lax.ppermute(later, "section", near)
    place = jnp.stack([chip ^ step for step in range(STEPS)] + [core])
    left, small = turned_factors(
        place, (first["left"], saved["left"], others_left, swap_cores(saved["left"]))
    )
    where = jnp.where(section == layers - 1, 2, jnp.where(section % RUN == RUN - 1, 1, 0))
    adjoint = (where[None], (front_near, hop), (front_far, far), final)
    right = attention_tick(*adjoint, wo, saved, left)
    own, sends = terms(left, small, [first["right"], right, others_right, swap_cores(right)])
    by_way = along(sends[2], (0, 1), (3, 2))
    middle = along(sends[2], (1, 2), (2, 1))
    beside = along(sends[0], (0, 1), (1, 0), (2, 3), (3, 2))
    outer = along(sends[1], (0, 2), (3, 1))
    parts, dj, back = stream_tick(saved["x"], adjoint, gain, w, right, saved, first, n, own)
    by_way, parts = lax.optimization_barrier((by_way, parts))
    both = (sends[1].astype(F32) + by_way.astype(F32)).astype(BF16)
    grads = [own, middle, beside, outer, along(both, (1, 3), (2, 0))]
    dx1 = output_tick(saved["x"], adjoint, saved["coef"], saved["bhl"], dj, back, both)
    parts, dx1 = lax.optimization_barrier((parts, dx1))
    parts = lax.all_to_all(parts, "dp", 0, 0)
    grad_map, grad_gain = finish_map(parts, n)
    grad_qkv, grad_out = finish_terms(grads, grad_map)
    dx0 = jnp.concatenate([first["dx_front"], first["dx_back"]], axis=1)
    sent = jnp.stack([jnp.transpose(dx0, (1, 0, 2)), jnp.transpose(dx1, (1, 0, 2))])[None]
    return (sent, grad_qkv[None], grad_out[None], grad_map.T[None], grad_gain)


def solution(mesh):
    return jax.shard_map(
        shards,
        mesh=mesh,
        in_specs=(
            P("section", None, "dp", None, None),
            P("section", "dp", None, None),
            P(None, "dp", None, None),
            P("section", None, "dp"),
            P("section", None, None),
            P("section", None),
            P("section", None, None),
            P("section", None, None),
        ),
        out_specs=(
            P("section", None, "dp", None, None),
            P("section", "dp", None),
            P("section", "dp", None),
            P("section", "dp", None),
            P("section", "dp"),
        ),
        check_vma=False,
    )
```

```python
import functools

import jax
import jax.numpy as jnp
from jax import lax
from jax.experimental import pallas as pl
from jax.experimental.pallas import tpu as pltpu
from jax.sharding import PartitionSpec as P

F32 = jnp.float32
BF16 = jnp.bfloat16
LANES = 4
D = 1024
T = 128
HEADS = 8
PAIRS = HEADS // 2
INNER = 512
SINK = 20
EPS = 1e-6
ROWS = 16
RUN = 4
FORWARD_COST = 1
FINISH_COST = 100
RIGHT = 3 * INNER + D
LEFT = D + INNER
FRONT = 80
NN = (((1,), (0,)), ((), ()))
NT = (((1,), (1,)), ((), ()))
TN = (((0,), (0,)), ((), ()))


def dot(a, b, dims=NN):
    return lax.dot_general(a, b, dims, preferred_element_type=F32)


def split(value):
    high = value.astype(BF16)
    return high, (value - high.astype(F32)).astype(BF16)


def iota(shape, axis):
    return lax.broadcasted_iota(jnp.int32, shape, axis)


def group_sum(block):
    block = block + pltpu.roll(block, 1, 0)
    return block + pltpu.roll(block, 2, 0)


def doubled(block):
    lower = iota(block.shape, 0) < 4
    turned = pltpu.roll(block, 4, 0)
    return jnp.where(lower, block, turned), jnp.where(lower, turned, block)


def tokens_first(rows):
    short = 128 - rows.shape[0]
    if short:
        rows = jnp.concatenate([rows, jnp.zeros((short, T), F32)], axis=0)
    return rows.T


def head_ones():
    return (iota((128, 128), 0) // 64 == iota((128, 128), 1) // 64).astype(BF16)


def head_mean(value, ones):
    high, low = split(value)
    return (dot(high, ones) + dot(low, ones)) * (1.0 / 64.0)


def half_masks():
    low = iota((1, 128), 1) < 64
    return low, [low.astype(F32).astype(BF16), (~low).astype(F32).astype(BF16)]


def stacked_map(bt_ref, bhl):
    high, low = split(jnp.concatenate([bt_ref[...], jnp.zeros((8, LANES * D), F32)], axis=0))
    bhl[0:32, :] = high
    bhl[32:64, :] = low


def forward(x, bhl, gain, w, wo, seg, s, wait):
    eye = iota((T, T), 0) == iota((T, T), 1)
    raw = jnp.zeros((64, T), F32)
    square = jnp.zeros((T, T), F32)
    for j in range(LANES):
        raw = raw + dot(bhl[:, j * D : (j + 1) * D], x[j], NT)
        square = square + dot(x[j], x[j], NT)
    mean = jnp.sum(jnp.where(eye, square, 0.0), axis=0, keepdims=True) * (1.0 / (LANES * D))
    inv = lax.rsqrt(mean + EPS)
    mc = (raw[0:24] + raw[32:56]) * inv
    s["mc"][...] = jnp.concatenate([mc, jnp.broadcast_to(inv, (8, T))], axis=0)
    lower = iota((8, T), 0) < 4
    gates = jax.nn.sigmoid(mc[0:8])
    gates = jnp.where(lower, gates, 2.0 * gates)
    first = doubled(jnp.exp(mc[8:16]))
    second = doubled(jnp.exp(mc[16:24]))

    def one_round(index, current):
        sums = [1.0 / group_sum(a) for a in current]
        current = [a * b for a, b in zip(current, sums)]
        for i in range(LANES):
            s["sink"][index, i] = current[i]
            s["sink"][index, 4 + i] = sums[i]
        total = 1.0 / ((current[0] + current[1]) + (current[2] + current[3]))
        current = [a * total for a in current]
        for i in range(LANES):
            s["sink"][index, 8 + i] = current[i]
        s["sink"][index, 12] = total
        return tuple(current)

    settled = lax.fori_loop(0, SINK, one_round, first + second)
    s["coef"][...] = tokens_first(
        jnp.concatenate(
            [
                gates,
                jnp.where(lower, settled[0], settled[1]),
                jnp.where(lower, settled[2], settled[3]),
            ],
            axis=0,
        )
    )

    def join_rows(block, _):
        rows = pl.ds(pl.multiple_of(block * ROWS, ROWS), ROWS)
        c = s["coef"][rows, :]
        joined = c[:, 0:1] * x[0, rows, :].astype(F32)
        for i in range(1, LANES):
            joined = joined + c[:, i : i + 1] * x[i, rows, :].astype(F32)
        r = lax.rsqrt(jnp.mean(joined * joined, axis=-1, keepdims=True) + EPS)
        s["joined"][rows, :] = joined
        s["r"][rows, :] = jnp.broadcast_to(r, (ROWS, 128))
        s["normed"][rows, :] = (joined * r * gain[...]).astype(BF16)
        return 0

    lax.fori_loop(0, T // ROWS, join_rows, 0)
    wait("w")
    projected = dot(s["normed"][...], w[...]).astype(BF16)
    s["proj"][...] = projected
    ones = head_ones()
    for at in range(2 * PAIRS):
        lanes = slice(at * 128, at * 128 + 128)
        wide = projected[:, lanes].astype(F32)
        scale = lax.rsqrt(head_mean(wide * wide, ones) + EPS)
        s["scale"][:, lanes] = scale
        s["qk"][:, lanes] = (wide * scale).astype(BF16)
    ids = jnp.broadcast_to(seg[...].astype(F32), (T, T))
    allowed = (ids == ids.T) & (iota((T, T), 1) <= iota((T, T), 0))
    low, masks = half_masks()
    for pair in range(PAIRS):
        lanes = slice(pair * 128, pair * 128 + 128)
        q = s["qk"][:, lanes]
        k = s["qk"][:, pl.ds(INNER + pair * 128, 128)]
        v = s["proj"][:, pl.ds(2 * INNER + pair * 128, 128)]
        parts = []
        for half in range(2):
            scores = dot(q * masks[half], k, NT) * 0.125
            free = jnp.where(allowed, jnp.exp(scores), 0.0)
            weights = free / jnp.sum(free, axis=-1, keepdims=True)
            s["weights"][2 * pair + half] = weights
            parts.append(dot(weights.astype(BF16), v))
        s["ctx"][:, lanes] = jnp.where(low, parts[0], parts[1]).astype(BF16)
    wait("wo")
    s["att"][...] = dot(s["ctx"][...], wo[...]).astype(BF16)


def diagonal(product, eye):
    return jnp.sum(jnp.where(eye, product, 0.0), axis=0, keepdims=True)


def by_sublane(rows):
    at = iota((8, T), 0) % 4
    block = jnp.broadcast_to(rows[3], (8, T))
    for k in range(3):
        block = jnp.where(at == k, jnp.broadcast_to(rows[k], (8, T)), block)
    return block


def adjoint_rows(g, s, out):
    def att_rows(block, _):
        rows = pl.ds(pl.multiple_of(block * ROWS, ROWS), ROWS)
        c = s["coef"][rows, :]
        total = c[:, 4:5] * g[0, rows, :].astype(F32)
        for i in range(1, LANES):
            total = total + c[:, 4 + i : 5 + i] * g[i, rows, :].astype(F32)
        out[rows, :] = total.astype(BF16)
        return 0

    lax.fori_loop(0, T // ROWS, att_rows, 0)


def attention_back(datt, wo, s, out):
    dctx = dot(datt[...], wo[...], NT).astype(BF16)
    low, masks = half_masks()
    ones = head_ones()

    def norm_back(dn, at):
        lanes = pl.ds(at * 128, 128)
        wide = s["proj"][:, lanes].astype(F32)
        scale = s["scale"][:, lanes]
        dn = dn.astype(BF16).astype(F32)
        moment = head_mean(dn * wide, ones)
        out[:, lanes] = (scale * (dn - wide * (scale * scale * moment))).astype(BF16)

    for pair in range(PAIRS):
        lanes = slice(pair * 128, pair * 128 + 128)
        q = s["qk"][:, pl.ds(pair * 128, 128)]
        key = s["qk"][:, pl.ds(INNER + pair * 128, 128)]
        v = s["proj"][:, pl.ds(2 * INNER + pair * 128, 128)]
        dc = dctx[:, lanes]
        dq, dk, dv = [], [], []
        for side in range(2):
            weights = s["weights"][2 * pair + side]
            dw = dot(dc * masks[side], v, NT).astype(BF16).astype(F32)
            dscore = weights * (dw - jnp.sum(dw * weights, axis=-1, keepdims=True)) * 0.125
            dq.append(dot(dscore.astype(BF16), key))
            dk.append(dot(dscore.T.astype(BF16), q))
            dv.append(dot(weights.T.astype(BF16), dc))
        out[:, pl.ds(2 * INNER + pair * 128, 128)] = jnp.where(low, dv[0], dv[1]).astype(BF16)
        norm_back(jnp.where(low, dq[0], dq[1]), pair)
        norm_back(jnp.where(low, dk[0], dk[1]), PAIRS + pair)


def stream_back(x, g, gain, w, s, o, t):
    eye = iota((T, T), 0) == iota((T, T), 1)
    t["dn"][...] = dot(o["dproj"][...], w[...], NT).astype(BF16)

    def joined_rows(block, total):
        rows = pl.ds(pl.multiple_of(block * ROWS, ROWS), ROWS)
        r = s["r"][rows, 0:1]
        joined = s["joined"][rows, :]
        dn = t["dn"][rows, :].astype(F32)
        total = total + jnp.sum(dn * (joined * r), axis=0, keepdims=True)
        scaled = dn * gain[...]
        moment = jnp.mean(scaled * joined, axis=-1, keepdims=True)
        t["dj"][rows, :] = r * scaled - joined * (r * r * r * moment)
        return total

    o["dgain"][...] = lax.fori_loop(0, T // ROWS, joined_rows, jnp.zeros((1, D), F32))

    dj = t["dj"][...].astype(BF16)
    pre = [diagonal(dot(dj, x[j], NT), eye) for j in range(LANES)]
    post = [diagonal(dot(g[i], s["att"][...], NT), eye) for i in range(LANES)]
    dmix = tuple(
        by_sublane([diagonal(dot(g[i], x[j], NT), eye) for j in range(LANES)])
        for i in range(LANES)
    )

    def one_round(step, current):
        index = SINK - 1 - step
        after = [s["sink"][index, 8 + i] for i in range(LANES)]
        pull = [a * b for a, b in zip(current, after)]
        pull = (pull[0] + pull[1]) + (pull[2] + pull[3])
        total = s["sink"][index, 12]
        current = [(a - pull) * total for a in current]
        between = [s["sink"][index, i] for i in range(LANES)]
        sums = [s["sink"][index, 4 + i] for i in range(LANES)]
        return tuple(
            (a - group_sum(a * b)) * c for a, b, c in zip(current, between, sums)
        )

    dmix = lax.fori_loop(0, SINK, one_round, dmix)
    lower = iota((8, T), 0) < 4
    mc = s["mc"][...]
    inv = mc[24:32]
    gates = jax.nn.sigmoid(mc[0:8])
    dgates = jnp.where(lower, by_sublane(pre), 2.0 * by_sublane(post))
    dmc = [
        dgates * gates * (1.0 - gates),
        jnp.where(lower, dmix[0], dmix[1]) * jnp.exp(mc[8:16]),
        jnp.where(lower, dmix[2], dmix[3]) * jnp.exp(mc[16:24]),
    ]
    dot_mc = dmc[0] * mc[0:8] + dmc[1] * mc[8:16] + dmc[2] * mc[16:24]
    dot_mc = jnp.sum(dot_mc, axis=0, keepdims=True)
    kappa = inv * inv * dot_mc * (1.0 / (LANES * D))
    scaled = jnp.concatenate([a * inv for a in dmc] + [jnp.zeros((8, T), F32)], axis=0)
    t["back"][...] = tokens_first(jnp.concatenate([scaled, scaled, kappa], axis=0))
    rows_first = scaled.astype(BF16)
    for j in range(LANES):
        o["dproj_map"][:, j * D : (j + 1) * D] = dot(rows_first, x[j])


def stream_out(x, g, bhl, s, t, put):
    lead = t["back"][:, 0:64].astype(BF16)
    for j in range(LANES):
        t["f"][j] = dot(lead, bhl[:, j * D : (j + 1) * D])

    def stream_rows(put, block, _):
        rows = pl.ds(pl.multiple_of(block * ROWS, ROWS), ROWS)
        c = s["coef"][rows, :]
        kap = t["back"][rows, 64:65]
        dj = t["dj"][rows, :]
        gs = [g[i, rows, :].astype(F32) for i in range(LANES)]
        for j in range(LANES):
            total = t["f"][j, rows, :] + c[:, j : j + 1] * dj - kap * x[j, rows, :].astype(F32)
            for i in range(LANES):
                at = 8 + LANES * i + j
                total = total + c[:, at : at + 1] * gs[i]
            put(block, j, total.astype(BF16))
        return 0

    for first, last, place in put:
        lax.fori_loop(first, last, functools.partial(stream_rows, place), 0)


SAVED = (
    ("mc", (32, T), F32),
    ("sink", (SINK, 13, 8, T), F32),
    ("coef", (T, 128), F32),
    ("joined", (T, D), F32),
    ("r", (T, 128), F32),
    ("proj", (T, 3 * INNER), BF16),
    ("scale", (T, 2 * INNER), F32),
    ("qk", (T, 2 * INNER), BF16),
    ("weights", (HEADS, T, T), F32),
    ("att", (T, D), BF16),
    ("bhl", (64, LANES * D), BF16),
)
LEFT_OUT = (("left", (T, LEFT), BF16),)
MAP = (("dproj_map", (32, LANES * D), F32), ("dgain", (1, D), F32))
CARRIED = (("dj", (T, D), F32), ("back", (T, 128), F32))
NORM = (("dn", (T, D), BF16),)
MAPPED = (("f", (LANES, T, D), F32),)
TEMPS = CARRIED + NORM + MAPPED
STREAMS = (("g", (LANES, T, D), BF16),)
VMEM = pl.BlockSpec(memory_space=pltpu.VMEM)
ANY = pl.BlockSpec(memory_space=pl.ANY)
SMEM = pl.BlockSpec(memory_space=pltpu.SMEM)


def struct(shape, dtype):
    return jax.ShapeDtypeStruct(shape, dtype)


def shapes(table):
    return [struct(shape, dtype) for _, shape, dtype in table]


def scratch(table):
    return [pltpu.VMEM(shape, dtype) for _, shape, dtype in table]


def names(table):
    return [name for name, _, _ in table]


def named(table, refs):
    return dict(zip(names(table), refs))


def call(body, outs, scratches, args, micros, name, specs=None):
    return pl.pallas_call(
        body,
        out_shape=outs,
        in_specs=specs or [VMEM] * len(args),
        out_specs=[VMEM] * len(outs),
        scratch_shapes=scratches,
        compiler_params=pltpu.CompilerParams(vmem_limit_bytes=56 * 1024 * 1024),
        cost_estimate=pl.CostEstimate(
            flops=micros * 1_000_000_000, bytes_accessed=micros * 2_000_000, transcendentals=0
        ),
        name=name,
    )(*args)


def brought(table, sources, rest, sem):
    buffers = named(table, rest)
    copies = {
        name: pltpu.make_async_copy(source, buffers[name], sem.at[k])
        for k, (name, source) in enumerate(zip(names(table), sources))
    }
    for copy in copies.values():
        copy.start()
    return buffers, lambda name: copies[name].wait()


def bring_adjoint(where, near, far, final, g, sem):
    parts = [g.at[:, pl.ds(0, FRONT), :], g.at[:, pl.ds(FRONT, T - FRONT), :]]
    last = [final.at[:, pl.ds(0, FRONT), :], final.at[:, pl.ds(FRONT, T - FRONT), :]]
    for case, sources in enumerate((near, far, last)):

        @pl.when(where[0] == case)
        def _(sources=sources):
            for k in range(2):
                pltpu.make_async_copy(sources[k], parts[k], sem.at[k]).start()

    def wait():
        for k in range(2):
            pltpu.make_async_copy(near[k], parts[k], sem.at[k]).wait()

    return wait


def factors(refs, right, left):
    if right is not None:
        refs["dproj"] = right.at[:, pl.ds(0, 3 * INNER)]
        refs["datt"] = right.at[:, pl.ds(3 * INNER, D)]
    if left is not None:
        refs["normed"] = left.at[:, pl.ds(0, D)]
        refs["ctx"] = left.at[:, pl.ds(D, INNER)]
    return refs


WEIGHTS = (("w", (D, 3 * INNER), BF16), ("wo", (INNER, D), BF16))
EARLY = (("x_rows", (T, LANES, D), BF16),)
LATE = EARLY + WEIGHTS + (("g_rows", (T, LANES, D), BF16),)
LANED = (("x", (LANES, T, D), BF16), ("g", (LANES, T, D), BF16))


def lanes_apart(source, out):
    def some_rows(block, _):
        rows = pl.ds(pl.multiple_of(block * ROWS, ROWS), ROWS)
        for j in range(LANES):
            out[j, rows, :] = source[rows, j, :]
        return 0

    lax.fori_loop(0, T // ROWS, some_rows, 0)


def whole_tick(x, g, seg, bt, gain, w, wo):
    outs = [
        ("dx_front", (LANES, FRONT, D), BF16),
        ("dx_back", (LANES, T - FRONT, D), BF16),
        ("right", (T, RIGHT), BF16),
        ("left", (T, LEFT), BF16),
        *MAP,
    ]

    def body(x, g, seg, bt, gain, w, wo, *rest):
        o = named(outs, rest)
        s = factors({}, None, o["left"])
        factors(o, o["right"], None)
        rest = rest[len(outs) :]
        s.update(named(SAVED, rest))
        t = named(TEMPS, rest[len(SAVED) :])
        rest = rest[len(SAVED) + len(TEMPS) :]
        buffers, wait = brought(LATE, (x.at[0], w, wo, g), rest, rest[-1])
        x_rows, w, wo, g_rows = (buffers[k] for k in names(LATE))
        laned = named(LANED, rest[len(LATE) :])
        wait("x_rows")
        lanes_apart(x_rows, laned["x"])
        x, g = laned["x"], laned["g"]
        stacked_map(bt, s["bhl"])
        forward(x, s["bhl"], gain, w, wo, seg.at[pl.ds(0, 1), :], s, wait)
        wait("g_rows")
        lanes_apart(g_rows, g)
        adjoint_rows(g, s, o["datt"])
        attention_back(o["datt"], wo, s, o["dproj"])

        def put_front(block, j, value):
            o["dx_front"][j, pl.ds(pl.multiple_of(block * ROWS, ROWS), ROWS), :] = value

        def put_back(block, j, value):
            at = pl.multiple_of(block * ROWS - FRONT, ROWS)
            o["dx_back"][j, pl.ds(at, ROWS), :] = value

        cut = FRONT // ROWS
        put = ((0, cut, put_front), (cut, T // ROWS, put_back))
        stream_back(x, g, gain, w, s, o, t)
        stream_out(x, g, s["bhl"], s, t, put)

    got = call(
        body,
        shapes(outs),
        scratch(SAVED)
        + scratch(TEMPS)
        + scratch(LATE)
        + scratch(LANED)
        + [pltpu.SemaphoreType.DMA((len(LATE),))],
        (x, g, seg, bt, gain, w, wo),
        20,
        "whole_tick",
        [ANY, ANY, VMEM, VMEM, VMEM, ANY, ANY],
    )
    return named(outs, got)


def forward_tick(x, seg, bt, gain, w, wo):
    table = SAVED + LEFT_OUT + LANED[:1]
    late = EARLY + WEIGHTS

    def body(x, seg, bt, gain, w, wo, *rest):
        s = named(table, rest)
        factors(s, None, s["left"])
        *rest, sem = rest[len(table) :]
        buffers, wait = brought(late, (x.at[1], w, wo), rest, sem)
        x_rows, w, wo = (buffers[k] for k in names(late))
        stacked_map(bt, s["bhl"])
        wait("x_rows")
        lanes_apart(x_rows, s["x"])
        forward(s["x"], s["bhl"], gain, w, wo, seg.at[pl.ds(1, 1), :], s, wait)

    got = call(
        body,
        shapes(table),
        scratch(late) + [pltpu.SemaphoreType.DMA((len(late),))],
        (x, seg, bt, gain, w, wo),
        FORWARD_COST,
        "forward_tick",
        [ANY, VMEM, VMEM, VMEM, ANY, ANY],
    )
    return named(table, got)


ATTENTION = [e for e in SAVED if e[0] in ("proj", "scale", "qk", "weights")]


def attention_tick(where, near, far, final, wo, saved, after):
    table = WEIGHTS[1:] + tuple(ATTENTION)

    def body(where, near0, near1, far0, far1, final, after, coef, *rest):
        sources, right, g = rest[: len(table)], rest[len(table)], rest[len(table) + 1]
        *buffers, g_sem, sem = rest[len(table) + 2 :]
        ready = bring_adjoint(where, (near0, near1), (far0, far1), final, g, g_sem)
        s, wait = brought(table, sources, buffers, sem)
        o = factors({}, right, None)
        ready()
        adjoint_rows(g, {"coef": coef}, o["datt"])
        for name in names(table):
            wait(name)
        attention_back(o["datt"], s["wo"], s, o["dproj"])

    args = (where, *near, *far, final, after, saved["coef"], wo, *[saved[k] for k in names(ATTENTION)])
    return call(
        body,
        [struct((T, RIGHT), BF16)],
        scratch(STREAMS)
        + scratch(table)
        + [pltpu.SemaphoreType.DMA((2,)), pltpu.SemaphoreType.DMA((len(table),))],
        args,
        5,
        "attention_tick",
        [SMEM] + [ANY] * 6 + [VMEM] + [ANY] * len(table),
    )[0]


REST = [e for e in SAVED if e[0] in ("mc", "sink", "joined", "r", "att")]


def stream_tick(x, adjoint, gain, w, right, saved, earlier, n, after):
    where, near, far, final = adjoint

    def body(where, near0, near1, far0, far1, final, after, x, gain, w, right, *rest):
        s = named(REST, rest)
        rest = rest[len(REST) :]
        first = named(MAP, rest)
        parts, *rest = rest[len(MAP) :]
        t = named(CARRIED, rest)
        rest = rest[len(CARRIED) :]
        o = named(MAP, rest)
        factors(o, right, None)
        rest = rest[len(MAP) :]
        t.update(named(NORM, rest))
        g, sem = rest[len(NORM) :]
        ready = bring_adjoint(where, (near0, near1), (far0, far1), final, g, sem)
        ready()
        stream_back(x, g, gain, w, s, o, t)
        width = LANES * D // n
        for d in range(n):
            cols = slice(d * width, d * width + width)
            proj = first["dproj_map"][:, cols] + o["dproj_map"][:, cols]
            lanes = slice(d * (D // n), (d + 1) * (D // n))
            total = first["dgain"][:, lanes] + o["dgain"][:, lanes]
            total = jnp.concatenate([total, jnp.zeros((1, width - D // n), F32)], axis=1)
            total = jnp.broadcast_to(total, (8, width))
            parts[d] = jnp.concatenate([proj[0:24], total], axis=0).astype(BF16)

    args = (where, *near, *far, final, after, x, gain, w, right)
    args += tuple(saved[k] for k in names(REST)) + tuple(earlier[k] for k in names(MAP))
    return call(
        body,
        [struct((n, 32, LANES * D // n), BF16)] + shapes(CARRIED),
        scratch(MAP) + scratch(NORM) + scratch(STREAMS) + [pltpu.SemaphoreType.DMA((2,))],
        args,
        6,
        "stream_tick",
        [SMEM] + [ANY] * 6 + [VMEM] * (4 + len(REST) + len(MAP)),
    )


def output_tick(x, adjoint, coef, bhl, dj, back, after):
    where, near, far, final = adjoint

    def body(where, near0, near1, far0, far1, final, after, x, coef, bhl, dj, back, dx, *rest):
        t = {"dj": dj, "back": back, "f": rest[0]}
        g, sem = rest[1:]
        ready = bring_adjoint(where, (near0, near1), (far0, far1), final, g, sem)
        ready()

        def put_rows(block, j, value):
            dx[j, pl.ds(pl.multiple_of(block * ROWS, ROWS), ROWS), :] = value

        stream_out(x, g, bhl, {"coef": coef}, t, ((0, T // ROWS, put_rows),))

    return call(
        body,
        [struct((LANES, T, D), BF16)],
        scratch(MAPPED) + scratch(STREAMS) + [pltpu.SemaphoreType.DMA((2,))],
        (where, *near, *far, final, after, x, coef, bhl, dj, back),
        5,
        "output_tick",
        [SMEM] + [ANY] * 6 + [VMEM] * 5,
    )[0]


STEPS = 4


def turned_factors(place, sides):
    rows, few = D // (2 * STEPS), INNER // (2 * STEPS)

    def body(place, *refs):
        refs, (left, small) = refs[:STEPS], refs[STEPS:]
        sides = [factors({}, None, side) for side in refs]
        even = place[STEPS] == 0
        for step in range(STEPS):
            chip = place[step]
            at = pl.multiple_of((2 * chip + place[STEPS]) * rows, rows)
            near = pl.multiple_of(chip * rows, rows)
            for k, side in enumerate(sides):
                tokens = slice(k * T, k * T + T)
                block = side["normed"][:, pl.ds(at, rows)].astype(F32).T
                left[step * rows : (step + 1) * rows, tokens] = block.astype(BF16)
                block = side["ctx"][:, pl.ds(near, rows)].astype(F32).T
                block = jnp.where(even, block[0:few], block[few:rows])
                small[step * few : (step + 1) * few, tokens] = block.astype(BF16)

    return call(
        body,
        [struct((STEPS * rows, STEPS * T), BF16), struct((STEPS * few, STEPS * T), BF16)],
        [],
        (place, *sides),
        FORWARD_COST,
        "turned_factors",
        [SMEM] + [VMEM] * STEPS,
    )


PACKED = 3 * INNER + D // 2


def terms(left, small, rights):
    rows, few = D // (2 * STEPS), INNER // (2 * STEPS)

    def body(left, small, *refs):
        rights, outs = refs[:STEPS], refs[STEPS:]

        def right(at):
            return jnp.concatenate([r[:, at : at + 256] for r in rights], axis=0)

        for at in range(0, 3 * INNER, 256):
            product = dot(left[...], right(at))
            for step in range(STEPS):
                part = product[step * rows : (step + 1) * rows]
                outs[step][:, at : at + 256] = part.astype(outs[step].dtype)
        for at in range(0, D, 256):
            product = dot(small[...], right(3 * INNER + at))
            top = few * (at // (D // 2))
            cols = 3 * INNER + at % (D // 2)
            for step in range(STEPS):
                part = product[step * few : (step + 1) * few]
                outs[step][top : top + few, cols : cols + 256] = part.astype(outs[step].dtype)

    own, *sends = call(
        body,
        [struct((rows, PACKED), F32)] + [struct((rows, PACKED), BF16)] * (STEPS - 1),
        [],
        (left, small, *rights),
        4,
        "terms",
    )
    return own, sends


def finish_terms(terms):
    few = INNER // (2 * STEPS)

    def body(*refs):
        *others, grad_qkv, grad_out = refs[1:]
        total = refs[0][...]
        for other in others:
            total = total + other[...].astype(F32)
        grad_qkv[...] = total[:, : 3 * INNER]
        grad_out[:, : D // 2] = total[:few, 3 * INNER :]
        grad_out[:, D // 2 :] = total[few:, 3 * INNER :]

    rows = terms[0].shape[0]
    outs = [struct((rows, 3 * INNER), F32), struct((few, D), F32)]
    return call(body, outs, [], terms, FINISH_COST, "finish_terms")


def finish_map(parts, n, after):
    width = LANES * D // n

    def body(parts, after, grad_map, grad_gain):
        total = parts[0].astype(F32)
        for d in range(1, n):
            total = total + parts[d].astype(F32)
        grad_map[...] = total[0:24]
        grad_gain[...] = total[24:25, 0 : D // n]

    return call(
        body,
        [struct((24, width), F32), struct((1, D // n), F32)],
        [],
        (parts, after),
        1,
        "finish_map",
        [VMEM, ANY],
    )


def shards(
    saved_entering_lanes,
    opening_adjoint,
    final_later_adjoint,
    document_labels,
    blend_linear_map,
    rescale_amplitude,
    attend_entry_maps,
    attend_exit_map,
):
    n = lax.axis_size("dp")
    layers = lax.axis_size("section")
    section = lax.axis_index("section")
    replica = lax.axis_index("dp")
    chip, core = replica // 2, replica % 2
    lanes_first = lambda a: jnp.transpose(a, (1, 0, 2))
    x = saved_entering_lanes[0]
    opening = opening_adjoint[0]
    final = lanes_first(final_later_adjoint[0])
    bt = blend_linear_map[0].T
    gain = rescale_amplitude
    w = attend_entry_maps[0]
    wo = attend_exit_map[0]

    def swap_cores(value):
        return lax.ppermute(value, "dp", [(i, i ^ 1) for i in range(n)])

    def along(value, *chips):
        route = [(2 * a + c, 2 * b + c) for a, b in chips for c in range(2)]
        return lax.ppermute(value, "dp", route)

    first = whole_tick(x, opening, document_labels[0], bt, gain, w, wo)

    near = [(s, s - 1) for s in range(1, layers) if s % RUN]
    cross = range(RUN, layers, RUN)
    hop = lax.ppermute(first["dx_back"], "section", near + [(s, s + RUN - 1) for s in cross])
    front_far = lax.ppermute(first["dx_front"], "section", [(s, s - 1) for s in cross])
    others_left, others_right = swap_cores(first["left"]), swap_cores(first["right"])
    saved = forward_tick(x, document_labels[0], bt, gain, w, wo)
    coming, later, _ = lax.optimization_barrier((hop, first["dx_front"], saved["coef"]))
    far = lax.ppermute(coming, "section", [(s + RUN - 1, s - 1) for s in cross])
    front_near = lax.ppermute(later, "section", near)
    place = jnp.stack([chip ^ step for step in range(STEPS)] + [core])
    left, small = turned_factors(
        place, (first["left"], saved["left"], others_left, swap_cores(saved["left"]))
    )
    where = jnp.where(section == layers - 1, 2, jnp.where(section % RUN == RUN - 1, 1, 0))
    adjoint = (where[None], (front_near, hop), (front_far, far), final)
    right = attention_tick(*adjoint, wo, saved, left)
    own, sends = terms(left, small, [first["right"], right, others_right, swap_cores(right)])
    by_way = along(sends[2], (0, 1), (3, 2))
    middle = along(sends[2], (1, 2), (2, 1))
    beside = along(sends[0], (0, 1), (1, 0), (2, 3), (3, 2))
    outer = along(sends[1], (0, 2), (3, 1))
    parts, dj, back = stream_tick(saved["x"], adjoint, gain, w, right, saved, first, n, own)
    by_way, parts = lax.optimization_barrier((by_way, parts))
    both = (sends[1].astype(F32) + by_way.astype(F32)).astype(BF16)
    grads = [own, middle, beside, outer, along(both, (1, 3), (2, 0))]
    dx1 = output_tick(saved["x"], adjoint, saved["coef"], saved["bhl"], dj, back, both)
    parts = lax.all_to_all(parts, "dp", 0, 0)
    grad_qkv, grad_out = finish_terms(grads)
    grad_map, grad_gain = finish_map(parts, n, grad_qkv)
    dx0 = jnp.concatenate([first["dx_front"], first["dx_back"]], axis=1)
    sent = jnp.stack([jnp.transpose(dx0, (1, 0, 2)), jnp.transpose(dx1, (1, 0, 2))])[None]
    return (sent, grad_qkv[None], grad_out[None], grad_map.T[None], grad_gain)


def solution(mesh):
    return jax.shard_map(
        shards,
        mesh=mesh,
        in_specs=(
            P("section", None, "dp", None, None),
            P("section", "dp", None, None),
            P(None, "dp", None, None),
            P("section", None, "dp"),
            P("section", None, None),
            P("section", None),
            P("section", None, None),
            P("section", None, None),
        ),
        out_specs=(
            P("section", None, "dp", None, None),
            P("section", "dp", None),
            P("section", "dp", None),
            P("section", "dp", None),
            P("section", "dp"),
        ),
        check_vma=False,
    )
```

```python
import functools

import jax
import jax.numpy as jnp
from jax import lax
from jax.experimental import pallas as pl
from jax.experimental.pallas import tpu as pltpu
from jax.sharding import PartitionSpec as P

F32 = jnp.float32
BF16 = jnp.bfloat16
LANES = 4
D = 1024
T = 128
HEADS = 8
PAIRS = HEADS // 2
INNER = 512
SINK = 20
EPS = 1e-6
ROWS = 16
RUN = 4
FORWARD_COST = 1
FINISH_COST = 100
RIGHT = 3 * INNER + D
LEFT = D + INNER
FRONT = 80
NN = (((1,), (0,)), ((), ()))
NT = (((1,), (1,)), ((), ()))
TN = (((0,), (0,)), ((), ()))


def dot(a, b, dims=NN):
    return lax.dot_general(a, b, dims, preferred_element_type=F32)


def split(value):
    high = value.astype(BF16)
    return high, (value - high.astype(F32)).astype(BF16)


def iota(shape, axis):
    return lax.broadcasted_iota(jnp.int32, shape, axis)


def group_sum(block):
    block = block + pltpu.roll(block, 1, 0)
    return block + pltpu.roll(block, 2, 0)


def doubled(block):
    lower = iota(block.shape, 0) < 4
    turned = pltpu.roll(block, 4, 0)
    return jnp.where(lower, block, turned), jnp.where(lower, turned, block)


def tokens_first(rows):
    short = 128 - rows.shape[0]
    if short:
        rows = jnp.concatenate([rows, jnp.zeros((short, T), F32)], axis=0)
    return rows.T


def head_ones():
    return (iota((128, 128), 0) // 64 == iota((128, 128), 1) // 64).astype(BF16)


def head_mean(value, ones):
    high, low = split(value)
    return (dot(high, ones) + dot(low, ones)) * (1.0 / 64.0)


def half_masks():
    low = iota((1, 128), 1) < 64
    return low, [low.astype(F32).astype(BF16), (~low).astype(F32).astype(BF16)]


def stacked_map(bt_ref, bhl):
    high, low = split(jnp.concatenate([bt_ref[...], jnp.zeros((8, LANES * D), F32)], axis=0))
    bhl[0:32, :] = high
    bhl[32:64, :] = low


def forward(x, bhl, gain, w, wo, seg, s, wait):
    eye = iota((T, T), 0) == iota((T, T), 1)
    raw = jnp.zeros((64, T), F32)
    square = jnp.zeros((T, T), F32)
    for j in range(LANES):
        raw = raw + dot(bhl[:, j * D : (j + 1) * D], x[j], NT)
        square = square + dot(x[j], x[j], NT)
    mean = jnp.sum(jnp.where(eye, square, 0.0), axis=0, keepdims=True) * (1.0 / (LANES * D))
    inv = lax.rsqrt(mean + EPS)
    mc = (raw[0:24] + raw[32:56]) * inv
    s["mc"][...] = jnp.concatenate([mc, jnp.broadcast_to(inv, (8, T))], axis=0)
    lower = iota((8, T), 0) < 4
    gates = jax.nn.sigmoid(mc[0:8])
    gates = jnp.where(lower, gates, 2.0 * gates)
    first = doubled(jnp.exp(mc[8:16]))
    second = doubled(jnp.exp(mc[16:24]))

    def one_round(index, current):
        sums = [1.0 / group_sum(a) for a in current]
        current = [a * b for a, b in zip(current, sums)]
        for i in range(LANES):
            s["sink"][index, i] = current[i]
            s["sink"][index, 4 + i] = sums[i]
        total = 1.0 / ((current[0] + current[1]) + (current[2] + current[3]))
        current = [a * total for a in current]
        for i in range(LANES):
            s["sink"][index, 8 + i] = current[i]
        s["sink"][index, 12] = total
        return tuple(current)

    settled = lax.fori_loop(0, SINK, one_round, first + second)
    s["coef"][...] = tokens_first(
        jnp.concatenate(
            [
                gates,
                jnp.where(lower, settled[0], settled[1]),
                jnp.where(lower, settled[2], settled[3]),
            ],
            axis=0,
        )
    )

    def join_rows(block, _):
        rows = pl.ds(pl.multiple_of(block * ROWS, ROWS), ROWS)
        c = s["coef"][rows, :]
        joined = c[:, 0:1] * x[0, rows, :].astype(F32)
        for i in range(1, LANES):
            joined = joined + c[:, i : i + 1] * x[i, rows, :].astype(F32)
        r = lax.rsqrt(jnp.mean(joined * joined, axis=-1, keepdims=True) + EPS)
        s["joined"][rows, :] = joined
        s["r"][rows, :] = jnp.broadcast_to(r, (ROWS, 128))
        s["normed"][rows, :] = (joined * r * gain[...]).astype(BF16)
        return 0

    lax.fori_loop(0, T // ROWS, join_rows, 0)
    wait("w")
    projected = dot(s["normed"][...], w[...]).astype(BF16)
    s["proj"][...] = projected
    ones = head_ones()
    for at in range(2 * PAIRS):
        lanes = slice(at * 128, at * 128 + 128)
        wide = projected[:, lanes].astype(F32)
        scale = lax.rsqrt(head_mean(wide * wide, ones) + EPS)
        s["scale"][:, lanes] = scale
        s["qk"][:, lanes] = (wide * scale).astype(BF16)
    ids = jnp.broadcast_to(seg[...].astype(F32), (T, T))
    allowed = (ids == ids.T) & (iota((T, T), 1) <= iota((T, T), 0))
    low, masks = half_masks()
    for pair in range(PAIRS):
        lanes = slice(pair * 128, pair * 128 + 128)
        q = s["qk"][:, lanes]
        k = s["qk"][:, pl.ds(INNER + pair * 128, 128)]
        v = s["proj"][:, pl.ds(2 * INNER + pair * 128, 128)]
        parts = []
        for half in range(2):
            scores = dot(q * masks[half], k, NT) * 0.125
            free = jnp.where(allowed, jnp.exp(scores), 0.0)
            weights = free / jnp.sum(free, axis=-1, keepdims=True)
            s["weights"][2 * pair + half] = weights
            parts.append(dot(weights.astype(BF16), v))
        s["ctx"][:, lanes] = jnp.where(low, parts[0], parts[1]).astype(BF16)
    wait("wo")
    s["att"][...] = dot(s["ctx"][...], wo[...]).astype(BF16)


def diagonal(product, eye):
    return jnp.sum(jnp.where(eye, product, 0.0), axis=0, keepdims=True)


def by_sublane(rows):
    at = iota((8, T), 0) % 4
    block = jnp.broadcast_to(rows[3], (8, T))
    for k in range(3):
        block = jnp.where(at == k, jnp.broadcast_to(rows[k], (8, T)), block)
    return block


def adjoint_rows(g, s, out):
    def att_rows(block, _):
        rows = pl.ds(pl.multiple_of(block * ROWS, ROWS), ROWS)
        c = s["coef"][rows, :]
        total = c[:, 4:5] * g[0, rows, :].astype(F32)
        for i in range(1, LANES):
            total = total + c[:, 4 + i : 5 + i] * g[i, rows, :].astype(F32)
        out[rows, :] = total.astype(BF16)
        return 0

    lax.fori_loop(0, T // ROWS, att_rows, 0)


def attention_back(datt, wo, s, out):
    dctx = dot(datt[...], wo[...], NT).astype(BF16)
    low, masks = half_masks()
    ones = head_ones()

    def norm_back(dn, at):
        lanes = pl.ds(at * 128, 128)
        wide = s["proj"][:, lanes].astype(F32)
        scale = s["scale"][:, lanes]
        dn = dn.astype(BF16).astype(F32)
        moment = head_mean(dn * wide, ones)
        out[:, lanes] = (scale * (dn - wide * (scale * scale * moment))).astype(BF16)

    for pair in range(PAIRS):
        lanes = slice(pair * 128, pair * 128 + 128)
        q = s["qk"][:, pl.ds(pair * 128, 128)]
        key = s["qk"][:, pl.ds(INNER + pair * 128, 128)]
        v = s["proj"][:, pl.ds(2 * INNER + pair * 128, 128)]
        dc = dctx[:, lanes]
        dq, dk, dv = [], [], []
        for side in range(2):
            weights = s["weights"][2 * pair + side]
            dw = dot(dc * masks[side], v, NT).astype(BF16).astype(F32)
            dscore = weights * (dw - jnp.sum(dw * weights, axis=-1, keepdims=True)) * 0.125
            dq.append(dot(dscore.astype(BF16), key))
            dk.append(dot(dscore.T.astype(BF16), q))
            dv.append(dot(weights.T.astype(BF16), dc))
        out[:, pl.ds(2 * INNER + pair * 128, 128)] = jnp.where(low, dv[0], dv[1]).astype(BF16)
        norm_back(jnp.where(low, dq[0], dq[1]), pair)
        norm_back(jnp.where(low, dk[0], dk[1]), PAIRS + pair)


def stream_back(x, g, gain, w, s, o, t):
    eye = iota((T, T), 0) == iota((T, T), 1)
    t["dn"][...] = dot(o["dproj"][...], w[...], NT).astype(BF16)

    def joined_rows(block, total):
        rows = pl.ds(pl.multiple_of(block * ROWS, ROWS), ROWS)
        r = s["r"][rows, 0:1]
        joined = s["joined"][rows, :]
        dn = t["dn"][rows, :].astype(F32)
        total = total + jnp.sum(dn * (joined * r), axis=0, keepdims=True)
        scaled = dn * gain[...]
        moment = jnp.mean(scaled * joined, axis=-1, keepdims=True)
        t["dj"][rows, :] = r * scaled - joined * (r * r * r * moment)
        return total

    o["dgain"][...] = lax.fori_loop(0, T // ROWS, joined_rows, jnp.zeros((1, D), F32))

    dj = t["dj"][...].astype(BF16)
    pre = [diagonal(dot(dj, x[j], NT), eye) for j in range(LANES)]
    post = [diagonal(dot(g[i], s["att"][...], NT), eye) for i in range(LANES)]
    dmix = tuple(
        by_sublane([diagonal(dot(g[i], x[j], NT), eye) for j in range(LANES)])
        for i in range(LANES)
    )

    def one_round(step, current):
        index = SINK - 1 - step
        after = [s["sink"][index, 8 + i] for i in range(LANES)]
        pull = [a * b for a, b in zip(current, after)]
        pull = (pull[0] + pull[1]) + (pull[2] + pull[3])
        total = s["sink"][index, 12]
        current = [(a - pull) * total for a in current]
        between = [s["sink"][index, i] for i in range(LANES)]
        sums = [s["sink"][index, 4 + i] for i in range(LANES)]
        return tuple(
            (a - group_sum(a * b)) * c for a, b, c in zip(current, between, sums)
        )

    dmix = lax.fori_loop(0, SINK, one_round, dmix)
    lower = iota((8, T), 0) < 4
    mc = s["mc"][...]
    inv = mc[24:32]
    gates = jax.nn.sigmoid(mc[0:8])
    dgates = jnp.where(lower, by_sublane(pre), 2.0 * by_sublane(post))
    dmc = [
        dgates * gates * (1.0 - gates),
        jnp.where(lower, dmix[0], dmix[1]) * jnp.exp(mc[8:16]),
        jnp.where(lower, dmix[2], dmix[3]) * jnp.exp(mc[16:24]),
    ]
    dot_mc = dmc[0] * mc[0:8] + dmc[1] * mc[8:16] + dmc[2] * mc[16:24]
    dot_mc = jnp.sum(dot_mc, axis=0, keepdims=True)
    kappa = inv * inv * dot_mc * (1.0 / (LANES * D))
    scaled = jnp.concatenate([a * inv for a in dmc] + [jnp.zeros((8, T), F32)], axis=0)
    t["back"][...] = tokens_first(jnp.concatenate([scaled, scaled, kappa], axis=0))
    rows_first = scaled.astype(BF16)
    for j in range(LANES):
        o["dproj_map"][:, j * D : (j + 1) * D] = dot(rows_first, x[j])


def stream_out(x, g, bhl, s, t, put):
    lead = t["back"][:, 0:64].astype(BF16)
    for j in range(LANES):
        t["f"][j] = dot(lead, bhl[:, j * D : (j + 1) * D])

    def stream_rows(put, block, _):
        rows = pl.ds(pl.multiple_of(block * ROWS, ROWS), ROWS)
        c = s["coef"][rows, :]
        kap = t["back"][rows, 64:65]
        dj = t["dj"][rows, :]
        gs = [g[i, rows, :].astype(F32) for i in range(LANES)]
        for j in range(LANES):
            total = t["f"][j, rows, :] + c[:, j : j + 1] * dj - kap * x[j, rows, :].astype(F32)
            for i in range(LANES):
                at = 8 + LANES * i + j
                total = total + c[:, at : at + 1] * gs[i]
            put(block, j, total.astype(BF16))
        return 0

    for first, last, place in put:
        lax.fori_loop(first, last, functools.partial(stream_rows, place), 0)


SAVED = (
    ("mc", (32, T), F32),
    ("sink", (SINK, 13, 8, T), F32),
    ("coef", (T, 128), F32),
    ("joined", (T, D), F32),
    ("r", (T, 128), F32),
    ("proj", (T, 3 * INNER), BF16),
    ("scale", (T, 2 * INNER), F32),
    ("qk", (T, 2 * INNER), BF16),
    ("weights", (HEADS, T, T), F32),
    ("att", (T, D), BF16),
    ("bhl", (64, LANES * D), BF16),
)
LEFT_OUT = (("left", (T, LEFT), BF16),)
MAP = (("dproj_map", (32, LANES * D), F32), ("dgain", (1, D), F32))
CARRIED = (("dj", (T, D), F32), ("back", (T, 128), F32))
NORM = (("dn", (T, D), BF16),)
MAPPED = (("f", (LANES, T, D), F32),)
TEMPS = CARRIED + NORM + MAPPED
STREAMS = (("g", (LANES, T, D), BF16),)
VMEM = pl.BlockSpec(memory_space=pltpu.VMEM)
ANY = pl.BlockSpec(memory_space=pl.ANY)
SMEM = pl.BlockSpec(memory_space=pltpu.SMEM)


def struct(shape, dtype):
    return jax.ShapeDtypeStruct(shape, dtype)


def shapes(table):
    return [struct(shape, dtype) for _, shape, dtype in table]


def scratch(table):
    return [pltpu.VMEM(shape, dtype) for _, shape, dtype in table]


def names(table):
    return [name for name, _, _ in table]


def named(table, refs):
    return dict(zip(names(table), refs))


def call(body, outs, scratches, args, micros, name, specs=None):
    return pl.pallas_call(
        body,
        out_shape=outs,
        in_specs=specs or [VMEM] * len(args),
        out_specs=[VMEM] * len(outs),
        scratch_shapes=scratches,
        compiler_params=pltpu.CompilerParams(vmem_limit_bytes=56 * 1024 * 1024),
        cost_estimate=pl.CostEstimate(
            flops=micros * 1_000_000_000, bytes_accessed=micros * 2_000_000, transcendentals=0
        ),
        name=name,
    )(*args)


def brought(table, sources, rest, sem):
    buffers = named(table, rest)
    copies = {
        name: pltpu.make_async_copy(source, buffers[name], sem.at[k])
        for k, (name, source) in enumerate(zip(names(table), sources))
    }
    for copy in copies.values():
        copy.start()
    return buffers, lambda name: copies[name].wait()


def bring_adjoint(where, near, far, final, g, sem):
    parts = [g.at[:, pl.ds(0, FRONT), :], g.at[:, pl.ds(FRONT, T - FRONT), :]]
    last = [final.at[:, pl.ds(0, FRONT), :], final.at[:, pl.ds(FRONT, T - FRONT), :]]
    for case, sources in enumerate((near, far, last)):

        @pl.when(where[0] == case)
        def _(sources=sources):
            for k in range(2):
                pltpu.make_async_copy(sources[k], parts[k], sem.at[k]).start()

    def wait():
        for k in range(2):
            pltpu.make_async_copy(near[k], parts[k], sem.at[k]).wait()

    return wait


def factors(refs, right, left):
    if right is not None:
        refs["dproj"] = right.at[:, pl.ds(0, 3 * INNER)]
        refs["datt"] = right.at[:, pl.ds(3 * INNER, D)]
    if left is not None:
        refs["normed"] = left.at[:, pl.ds(0, D)]
        refs["ctx"] = left.at[:, pl.ds(D, INNER)]
    return refs


WEIGHTS = (("w", (D, 3 * INNER), BF16), ("wo", (INNER, D), BF16))
EARLY = (("x_rows", (T, LANES, D), BF16),)
LATE = EARLY + WEIGHTS + (("g_rows", (T, LANES, D), BF16),)
LANED = (("x", (LANES, T, D), BF16), ("g", (LANES, T, D), BF16))


def lanes_apart(source, out):
    def some_rows(block, _):
        rows = pl.ds(pl.multiple_of(block * ROWS, ROWS), ROWS)
        for j in range(LANES):
            out[j, rows, :] = source[rows, j, :]
        return 0

    lax.fori_loop(0, T // ROWS, some_rows, 0)


def whole_tick(x, g, seg, bt, gain, w, wo):
    outs = [
        ("dx_front", (LANES, FRONT, D), BF16),
        ("dx_back", (LANES, T - FRONT, D), BF16),
        ("right", (T, RIGHT), BF16),
        ("left", (T, LEFT), BF16),
        *MAP,
    ]

    def body(x, g, seg, bt, gain, w, wo, *rest):
        o = named(outs, rest)
        s = factors({}, None, o["left"])
        factors(o, o["right"], None)
        rest = rest[len(outs) :]
        s.update(named(SAVED, rest))
        t = named(TEMPS, rest[len(SAVED) :])
        rest = rest[len(SAVED) + len(TEMPS) :]
        buffers, wait = brought(LATE, (x.at[0], w, wo, g), rest, rest[-1])
        x_rows, w, wo, g_rows = (buffers[k] for k in names(LATE))
        laned = named(LANED, rest[len(LATE) :])
        wait("x_rows")
        lanes_apart(x_rows, laned["x"])
        x, g = laned["x"], laned["g"]
        stacked_map(bt, s["bhl"])
        forward(x, s["bhl"], gain, w, wo, seg.at[pl.ds(0, 1), :], s, wait)
        wait("g_rows")
        lanes_apart(g_rows, g)
        adjoint_rows(g, s, o["datt"])
        attention_back(o["datt"], wo, s, o["dproj"])

        def put_front(block, j, value):
            o["dx_front"][j, pl.ds(pl.multiple_of(block * ROWS, ROWS), ROWS), :] = value

        def put_back(block, j, value):
            at = pl.multiple_of(block * ROWS - FRONT, ROWS)
            o["dx_back"][j, pl.ds(at, ROWS), :] = value

        cut = FRONT // ROWS
        put = ((0, cut, put_front), (cut, T // ROWS, put_back))
        stream_back(x, g, gain, w, s, o, t)
        stream_out(x, g, s["bhl"], s, t, put)

    got = call(
        body,
        shapes(outs),
        scratch(SAVED)
        + scratch(TEMPS)
        + scratch(LATE)
        + scratch(LANED)
        + [pltpu.SemaphoreType.DMA((len(LATE),))],
        (x, g, seg, bt, gain, w, wo),
        20,
        "whole_tick",
        [ANY, ANY, VMEM, VMEM, VMEM, ANY, ANY],
    )
    return named(outs, got)


def forward_tick(x, seg, bt, gain, w, wo):
    table = SAVED + LEFT_OUT + LANED[:1]
    late = EARLY + WEIGHTS

    def body(x, seg, bt, gain, w, wo, *rest):
        s = named(table, rest)
        factors(s, None, s["left"])
        *rest, sem = rest[len(table) :]
        buffers, wait = brought(late, (x.at[1], w, wo), rest, sem)
        x_rows, w, wo = (buffers[k] for k in names(late))
        stacked_map(bt, s["bhl"])
        wait("x_rows")
        lanes_apart(x_rows, s["x"])
        forward(s["x"], s["bhl"], gain, w, wo, seg.at[pl.ds(1, 1), :], s, wait)

    got = call(
        body,
        shapes(table),
        scratch(late) + [pltpu.SemaphoreType.DMA((len(late),))],
        (x, seg, bt, gain, w, wo),
        FORWARD_COST,
        "forward_tick",
        [ANY, VMEM, VMEM, VMEM, ANY, ANY],
    )
    return named(table, got)


ATTENTION = [e for e in SAVED if e[0] in ("proj", "scale", "qk", "weights")]


def attention_tick(where, near, far, final, wo, saved, after):
    table = WEIGHTS[1:] + tuple(ATTENTION)

    def body(where, near0, near1, far0, far1, final, after, coef, *rest):
        sources, right, g = rest[: len(table)], rest[len(table)], rest[len(table) + 1]
        *buffers, g_sem, sem = rest[len(table) + 2 :]
        ready = bring_adjoint(where, (near0, near1), (far0, far1), final, g, g_sem)
        s, wait = brought(table, sources, buffers, sem)
        o = factors({}, right, None)
        ready()
        adjoint_rows(g, {"coef": coef}, o["datt"])
        for name in names(table):
            wait(name)
        attention_back(o["datt"], s["wo"], s, o["dproj"])

    args = (where, *near, *far, final, after, saved["coef"], wo, *[saved[k] for k in names(ATTENTION)])
    return call(
        body,
        [struct((T, RIGHT), BF16)],
        scratch(STREAMS)
        + scratch(table)
        + [pltpu.SemaphoreType.DMA((2,)), pltpu.SemaphoreType.DMA((len(table),))],
        args,
        5,
        "attention_tick",
        [SMEM] + [ANY] * 6 + [VMEM] + [ANY] * len(table),
    )[0]


REST = [e for e in SAVED if e[0] in ("mc", "sink", "joined", "r", "att")]


def stream_tick(x, adjoint, gain, w, right, saved, earlier, n, after):
    where, near, far, final = adjoint

    def body(where, near0, near1, far0, far1, final, after, x, gain, w, right, *rest):
        s = named(REST, rest)
        rest = rest[len(REST) :]
        first = named(MAP, rest)
        parts, *rest = rest[len(MAP) :]
        t = named(CARRIED, rest)
        rest = rest[len(CARRIED) :]
        o = named(MAP, rest)
        factors(o, right, None)
        rest = rest[len(MAP) :]
        t.update(named(NORM, rest))
        g, sem = rest[len(NORM) :]
        ready = bring_adjoint(where, (near0, near1), (far0, far1), final, g, sem)
        ready()
        stream_back(x, g, gain, w, s, o, t)
        width = LANES * D // n
        for d in range(n):
            cols = slice(d * width, d * width + width)
            proj = first["dproj_map"][:, cols] + o["dproj_map"][:, cols]
            lanes = slice(d * (D // n), (d + 1) * (D // n))
            total = first["dgain"][:, lanes] + o["dgain"][:, lanes]
            total = jnp.concatenate([total, jnp.zeros((1, width - D // n), F32)], axis=1)
            total = jnp.broadcast_to(total, (8, width))
            parts[d] = jnp.concatenate([proj[0:24], total], axis=0).astype(BF16)

    args = (where, *near, *far, final, after, x, gain, w, right)
    args += tuple(saved[k] for k in names(REST)) + tuple(earlier[k] for k in names(MAP))
    return call(
        body,
        [struct((n, 32, LANES * D // n), BF16)] + shapes(CARRIED),
        scratch(MAP) + scratch(NORM) + scratch(STREAMS) + [pltpu.SemaphoreType.DMA((2,))],
        args,
        6,
        "stream_tick",
        [SMEM] + [ANY] * 6 + [VMEM] * (4 + len(REST) + len(MAP)),
    )


def output_tick(x, adjoint, coef, bhl, dj, back, after):
    where, near, far, final = adjoint

    def body(where, near0, near1, far0, far1, final, after, x, coef, bhl, dj, back, dx, *rest):
        t = {"dj": dj, "back": back, "f": rest[0]}
        g, sem = rest[1:]
        ready = bring_adjoint(where, (near0, near1), (far0, far1), final, g, sem)
        ready()

        def put_rows(block, j, value):
            dx[j, pl.ds(pl.multiple_of(block * ROWS, ROWS), ROWS), :] = value

        stream_out(x, g, bhl, {"coef": coef}, t, ((0, T // ROWS, put_rows),))

    return call(
        body,
        [struct((LANES, T, D), BF16)],
        scratch(MAPPED) + scratch(STREAMS) + [pltpu.SemaphoreType.DMA((2,))],
        (where, *near, *far, final, after, x, coef, bhl, dj, back),
        5,
        "output_tick",
        [SMEM] + [ANY] * 6 + [VMEM] * 5,
    )[0]


STEPS = 4


def turned_factors(place, sides):
    rows, few = D // (2 * STEPS), INNER // (2 * STEPS)

    def body(place, *refs):
        refs, (left, small) = refs[:STEPS], refs[STEPS:]
        sides = [factors({}, None, side) for side in refs]
        even = place[STEPS] == 0
        for step in range(STEPS):
            chip = place[step]
            at = pl.multiple_of((2 * chip + place[STEPS]) * rows, rows)
            near = pl.multiple_of(chip * rows, rows)
            for k, side in enumerate(sides):
                tokens = slice(k * T, k * T + T)
                block = side["normed"][:, pl.ds(at, rows)].astype(F32).T
                left[step * rows : (step + 1) * rows, tokens] = block.astype(BF16)
                block = side["ctx"][:, pl.ds(near, rows)].astype(F32).T
                block = jnp.where(even, block[0:few], block[few:rows])
                small[step * few : (step + 1) * few, tokens] = block.astype(BF16)

    return call(
        body,
        [struct((STEPS * rows, STEPS * T), BF16), struct((STEPS * few, STEPS * T), BF16)],
        [],
        (place, *sides),
        FORWARD_COST,
        "turned_factors",
        [SMEM] + [VMEM] * STEPS,
    )


PACKED = 3 * INNER + D // 2


def terms(left, small, rights):
    rows, few = D // (2 * STEPS), INNER // (2 * STEPS)

    def body(left, small, *refs):
        rights, outs = refs[:STEPS], refs[STEPS:]

        def right(at):
            return jnp.concatenate([r[:, at : at + 256] for r in rights], axis=0)

        for at in range(0, 3 * INNER, 256):
            product = dot(left[...], right(at))
            for step in range(STEPS):
                part = product[step * rows : (step + 1) * rows]
                outs[step][:, at : at + 256] = part.astype(outs[step].dtype)
        for at in range(0, D, 256):
            product = dot(small[...], right(3 * INNER + at))
            top = few * (at // (D // 2))
            cols = 3 * INNER + at % (D // 2)
            for step in range(STEPS):
                part = product[step * few : (step + 1) * few]
                outs[step][top : top + few, cols : cols + 256] = part.astype(outs[step].dtype)

    own, *sends = call(
        body,
        [struct((rows, PACKED), BF16)] * STEPS,
        [],
        (left, small, *rights),
        4,
        "terms",
    )
    return own, sends


def finish_terms(terms):
    few = INNER // (2 * STEPS)

    def body(*refs):
        *others, grad_qkv, grad_out = refs[1:]
        total = refs[0][...].astype(F32)
        for other in others:
            total = total + other[...].astype(F32)
        grad_qkv[...] = total[:, : 3 * INNER]
        grad_out[:, : D // 2] = total[:few, 3 * INNER :]
        grad_out[:, D // 2 :] = total[few:, 3 * INNER :]

    rows = terms[0].shape[0]
    outs = [struct((rows, 3 * INNER), F32), struct((few, D), F32)]
    return call(body, outs, [], terms, FINISH_COST, "finish_terms")


def finish_map(parts, n, after):
    width = LANES * D // n

    def body(parts, after, grad_map, grad_gain):
        total = parts[0].astype(F32)
        for d in range(1, n):
            total = total + parts[d].astype(F32)
        grad_map[...] = total[0:24]
        grad_gain[...] = total[24:25, 0 : D // n]

    return call(
        body,
        [struct((24, width), F32), struct((1, D // n), F32)],
        [],
        (parts, after),
        1,
        "finish_map",
        [VMEM, ANY],
    )


def shards(
    saved_entering_lanes,
    opening_adjoint,
    final_later_adjoint,
    document_labels,
    blend_linear_map,
    rescale_amplitude,
    attend_entry_maps,
    attend_exit_map,
):
    n = lax.axis_size("dp")
    layers = lax.axis_size("section")
    section = lax.axis_index("section")
    replica = lax.axis_index("dp")
    chip, core = replica // 2, replica % 2
    lanes_first = lambda a: jnp.transpose(a, (1, 0, 2))
    x = saved_entering_lanes[0]
    opening = opening_adjoint[0]
    final = lanes_first(final_later_adjoint[0])
    bt = blend_linear_map[0].T
    gain = rescale_amplitude
    w = attend_entry_maps[0]
    wo = attend_exit_map[0]

    def swap_cores(value):
        return lax.ppermute(value, "dp", [(i, i ^ 1) for i in range(n)])

    def along(value, *chips):
        route = [(2 * a + c, 2 * b + c) for a, b in chips for c in range(2)]
        return lax.ppermute(value, "dp", route)

    first = whole_tick(x, opening, document_labels[0], bt, gain, w, wo)

    near = [(s, s - 1) for s in range(1, layers) if s % RUN]
    cross = range(RUN, layers, RUN)
    hop = lax.ppermute(first["dx_back"], "section", near + [(s, s + RUN - 1) for s in cross])
    front_far = lax.ppermute(first["dx_front"], "section", [(s, s - 1) for s in cross])
    others_left, others_right = swap_cores(first["left"]), swap_cores(first["right"])
    saved = forward_tick(x, document_labels[0], bt, gain, w, wo)
    coming, later, _ = lax.optimization_barrier((hop, first["dx_front"], saved["coef"]))
    far = lax.ppermute(coming, "section", [(s + RUN - 1, s - 1) for s in cross])
    front_near = lax.ppermute(later, "section", near)
    place = jnp.stack([chip ^ step for step in range(STEPS)] + [core])
    left, small = turned_factors(
        place, (first["left"], saved["left"], others_left, swap_cores(saved["left"]))
    )
    where = jnp.where(section == layers - 1, 2, jnp.where(section % RUN == RUN - 1, 1, 0))
    adjoint = (where[None], (front_near, hop), (front_far, far), final)
    right = attention_tick(*adjoint, wo, saved, left)
    own, sends = terms(left, small, [first["right"], right, others_right, swap_cores(right)])
    by_way = along(sends[2], (0, 1), (3, 2))
    middle = along(sends[2], (1, 2), (2, 1))
    beside = along(sends[0], (0, 1), (1, 0), (2, 3), (3, 2))
    outer = along(sends[1], (0, 2), (3, 1))
    parts, dj, back = stream_tick(saved["x"], adjoint, gain, w, right, saved, first, n, own)
    by_way, parts = lax.optimization_barrier((by_way, parts))
    both = (sends[1].astype(F32) + by_way.astype(F32)).astype(BF16)
    grads = [own, middle, beside, outer, along(both, (1, 3), (2, 0))]
    dx1 = output_tick(saved["x"], adjoint, saved["coef"], saved["bhl"], dj, back, both)
    parts = lax.all_to_all(parts, "dp", 0, 0)
    grad_qkv, grad_out = finish_terms(grads)
    grad_map, grad_gain = finish_map(parts, n, grad_qkv)
    dx0 = jnp.concatenate([first["dx_front"], first["dx_back"]], axis=1)
    sent = jnp.stack([jnp.transpose(dx0, (1, 0, 2)), jnp.transpose(dx1, (1, 0, 2))])[None]
    return (sent, grad_qkv[None], grad_out[None], grad_map.T[None], grad_gain)


def solution(mesh):
    return jax.shard_map(
        shards,
        mesh=mesh,
        in_specs=(
            P("section", None, "dp", None, None),
            P("section", "dp", None, None),
            P(None, "dp", None, None),
            P("section", None, "dp"),
            P("section", None, None),
            P("section", None),
            P("section", None, None),
            P("section", None, None),
        ),
        out_specs=(
            P("section", None, "dp", None, None),
            P("section", "dp", None),
            P("section", "dp", None),
            P("section", "dp", None),
            P("section", "dp"),
        ),
        check_vma=False,
    )
```
